32 devices in a mesh: row: 4 (over z), col: 8 (over y, x, core).
Axes of the slice: x: 2, y: 2, z: 4, core: 2. Of those that a mesh axis runs over, the one named last changes fastest.
Arguments:
- lead: bfloat16 [2, 1024, 2048], P(None, 'row'), may hold values from -0.5 to 28, as said below
- panel: float32 [2048, 2048], P(('row', 'col')), may hold values from -6 to 6
- row_present: int32 [16], replicated, may hold values 0 or 1
- trailing: float32 [2048, 2048], P('row', 'col'), may hold values from -6 to 6
Outputs:
- updated: float32 [2048, 2048], P('row', 'col')
- factor_rows: bfloat16 [2048, 2048], P(('row', 'col'))
The draws below stay inside these ranges and needn't reach their ends.
Inputs may be any that keep to these rules, and one draw needn't show every extreme that they name: `lead`: the two halves stacked row after row form a symmetric positive definite matrix of order 2048.
All inputs are finite; a program needn't handle non-finite values.
Results may differ from the reference program's by a relative error of at most 0.0013.
Values may be sent and summed in bfloat16 or wider, within the bound.
No kernel may reach another device: no remote copies, remote signals or barrier semaphores. Data moves between devices by JAX's collectives and lax.ppermute only.
A program may use at most 128 MiB of HBM per device.

```python
import jax
import jax.numpy as jnp
from jax import lax

PANEL = 1024
TILE = 128
LEAD = 2048
ROWS = 2048
TILES = 16


def draw_lead(key, part):
    key_band, key_far, key_diag, key_cross = jax.random.split(key, 4)
    positions = jnp.arange(LEAD)
    row_pos = positions[:, None]
    col_pos = positions[None, :]
    distance = jnp.abs(row_pos - col_pos)
    band_vals = jax.random.uniform(key_band, (LEAD, LEAD), jnp.float32, -0.5, 0.5)
    far_raw = jax.random.uniform(key_far, (LEAD, LEAD), jnp.float32, -1.0, 1.0)
    cross_vals = jax.random.uniform(key_cross, (LEAD, LEAD), jnp.float32, -0.3, 0.3)
    far_vals = far_raw * 0.1
    across = row_pos // PANEL != col_pos // PANEL
    outside = jnp.where(across, cross_vals, far_vals)
    offdiag = jnp.where(distance <= 8, band_vals, outside)
    symmetric = jnp.where(row_pos > col_pos, offdiag, offdiag.T)
    diag_vals = 22.0 + 6.0 * jax.random.uniform(key_diag, (LEAD,), jnp.float32)
    matrix = jnp.where(row_pos == col_pos, diag_vals[:, None], symmetric)
    return matrix.reshape(2, PANEL, LEAD).astype(jnp.bfloat16)


def place_ends(drawn, key, smallest, top_value):
    extent = drawn.shape
    spot = [jax.random.randint(jax.random.fold_in(key, axis), (), 0, extent[axis]) for axis in range(len(extent))]
    drawn = drawn.at[tuple(spot)].set(smallest)
    longest = extent.index(max(extent))
    spot[longest] = (spot[longest] + 1) % extent[longest]
    return drawn.at[tuple(spot)].set(top_value)


def steps_of(rng, dims, cuts, low, top_value):
    loudness, own = 1.0, jax.random.fold_in(rng, 6)
    for position, shards_of in cuts:
        heights = jnp.exp(jax.random.uniform(jax.random.fold_in(own, position), (shards_of,), jnp.float32, low / len(cuts), top_value / len(cuts)))
        loudness = loudness * jnp.repeat(heights, dims[position] // shards_of).reshape([-1 if axis == position else 1 for axis in range(len(dims))])
    return loudness


def scatter_about(own_key, extent, spread, most, cuts=(), held_as=jnp.bfloat16):
    result = jax.random.normal(own_key, extent, jnp.float32) * spread
    if len(cuts) > 0:
        result = steps_of(own_key, extent, cuts, -0.22, 0.18) * result
    return jnp.clip(result, min=-most, max=most).astype(held_as)


def setup_inputs(seed: int = 0) -> dict:
    key_of = jax.random.split(jax.random.key(seed), 5)
    return {
        "lead": draw_lead(jax.random.fold_in(key_of[4], 71), 0),
        "panel": scatter_about(key_of[1], (ROWS, LEAD), 1.0, 6.0, ((0, 32),), jnp.float32),
        "row_present": place_ends((jax.random.randint(key_of[2], (TILES,), 0, 4) < 3).astype(jnp.int32), jax.random.fold_in(key_of[2], 1), 0, 1),
        "trailing": scatter_about(key_of[3], (ROWS, ROWS), 1.0, 6.0, ((0, 4), (1, 8)), jnp.float32),
    }


def solve_right(factor, right_side):
    return lax.linalg.triangular_solve(factor, right_side, left_side=False, lower=True, transpose_a=True)

def reference(lead, panel, row_present, trailing):
    first_block = lead[0, :, :PANEL].astype(jnp.float32)
    first_factor = jnp.linalg.cholesky(first_block)
    coupling = solve_right(first_factor, lead[1, :, :PANEL].astype(jnp.float32)).astype(jnp.bfloat16)
    schur_block = lead[1, :, PANEL:].astype(jnp.float32) - jnp.dot(coupling.astype(jnp.float32), coupling.T.astype(jnp.float32), preferred_element_type=jnp.float32)
    second_factor = jnp.linalg.cholesky(schur_block)
    rowmask = jnp.repeat(row_present, TILE).astype(jnp.float32)
    masked = panel * rowmask[:, None]
    first_cols = solve_right(first_factor, masked[:, :PANEL]).astype(jnp.bfloat16)
    remainder = masked[:, PANEL:] - jnp.dot(first_cols.astype(jnp.float32), coupling.T.astype(jnp.float32), preferred_element_type=jnp.float32)
    second_cols = solve_right(second_factor, remainder).astype(jnp.bfloat16)
    factor_rows = jnp.concatenate([first_cols, second_cols], axis=1)
    updated = trailing - jnp.dot(factor_rows.astype(jnp.float32), factor_rows.T.astype(jnp.float32), preferred_element_type=jnp.float32)
    return (updated, factor_rows)
```

```python
import functools

import jax
import jax.numpy as jnp
from jax import lax
from jax.experimental import pallas as pl
from jax.experimental.pallas import tpu as pltpu
from jax.sharding import PartitionSpec as P

TILE = 128
BLOCK = 128
SLAB = 8
VMEM_BYTES = 48 * 1024 * 1024


def contract(left_rows, right_rows):
    return lax.dot_general(
        left_rows, right_rows, (((1,), (1,)), ((), ())), preferred_element_type=jnp.float32
    )


def split(value):
    high = value.astype(jnp.bfloat16)
    return high, (value - high.astype(jnp.float32)).astype(jnp.bfloat16)


def contract_split(left, right):
    return (
        contract(left[0], right[0]) + contract(left[0], right[1]) + contract(left[1], right[0])
    )


def factor_block(rows, put):
    shape = (SLAB, BLOCK)
    lane = lax.broadcasted_iota(jnp.int32, shape, 1)
    sub = lax.broadcasted_iota(jnp.int32, shape, 0)

    def spread(value, row):
        return jnp.broadcast_to(value[row : row + 1, :], shape)

    rows = list(rows)
    for s in range(len(rows)):
        low = SLAB * s
        inside = (lane >= low) & (lane < low + SLAB)
        now = rows[s]
        col = [jnp.broadcast_to(now[:, low + t : low + t + 1], shape) for t in range(SLAB)]
        value = jnp.where(inside, jnp.where(lane - low == sub, 1.0, 0.0), now)
        inverse = jnp.zeros(shape, jnp.float32)
        for t in range(0, SLAB, 2):
            c0, c1 = col[t], col[t + 1]
            a, b, c = spread(c0, t), spread(c0, t + 1), spread(c1, t + 1)
            det = a * c - b * b
            over = 1.0 / det
            root_a = lax.rsqrt(a)
            root_c = lax.rsqrt(det * (root_a * root_a))
            v0, v1 = spread(value, t), spread(value, t + 1)
            second = (v1 - v0 * (b * root_a * root_a)) * root_c
            inverse = jnp.where(sub == t, v0 * root_a, jnp.where(sub == t + 1, second, inverse))
            here = (sub == t) | (sub == t + 1)
            c0 = jnp.where(sub == t, -1.0, jnp.where(sub == t + 1, 0.0, c0))
            c1 = jnp.where(sub == t, 0.0, jnp.where(sub == t + 1, -1.0, c1))
            m0 = (c0 * c - c1 * b) * over
            m1 = (c1 * a - c0 * b) * over
            for u in range(t + 2, SLAB):
                x = col[u]
                col[u] = jnp.where(here, 0.0, x) - m0 * spread(x, t) - m1 * spread(x, t + 1)
            value = jnp.where(here, 0.0, value) - m0 * v0 - m1 * v1
        put(s, jnp.where(lane <= sub + low, inverse, 0.0))
        if s + 1 < len(rows):
            lines = [spread(value, t) for t in range(SLAB)]
            for i in range(s + 1, len(rows)):
                x = rows[i]
                total = jnp.where(inside, 0.0, x)
                for t in range(SLAB):
                    total = total - jnp.broadcast_to(x[:, low + t : low + t + 1], shape) * lines[t]
                rows[i] = total


def factor_kernel(blocks, block_ref, high_ref, low_ref, inv_high_ref, inv_low_ref, held, inv):
    held[...] = block_ref[...].astype(jnp.float32)
    for k in range(blocks):
        here = slice(k * BLOCK, (k + 1) * BLOCK)
        rows = [
            held[k * BLOCK + SLAB * s : k * BLOCK + SLAB * (s + 1), here]
            for s in range(BLOCK // SLAB)
        ]

        def put(s, value):
            inv[SLAB * s : SLAB * (s + 1), :] = value

        factor_block(rows, put)
        inverse = split(inv[...])
        inv_high_ref[here, :] = inverse[0]
        inv_low_ref[here, :] = inverse[1]
        if k + 1 < blocks:
            below = slice((k + 1) * BLOCK, blocks * BLOCK)
            factor = split(contract_split(split(held[below, here]), inverse))
            high_ref[below, here] = factor[0]
            low_ref[below, here] = factor[1]
            for j in range(k + 1, blocks):
                start = (j - k - 1) * BLOCK
                left = (factor[0][start:], factor[1][start:])
                right = (factor[0][start : start + BLOCK], factor[1][start : start + BLOCK])
                there = (slice(j * BLOCK, blocks * BLOCK), slice(j * BLOCK, (j + 1) * BLOCK))
                held[there] = held[there] - contract_split(left, right)


def factor(block, name):
    order = block.shape[0]
    whole = jax.ShapeDtypeStruct((order, order), jnp.bfloat16)
    diagonal = jax.ShapeDtypeStruct((order, BLOCK), jnp.bfloat16)
    return pl.pallas_call(
        functools.partial(factor_kernel, order // BLOCK),
        out_shape=(whole, whole, diagonal, diagonal),
        scratch_shapes=[
            pltpu.VMEM((order, order), jnp.float32),
            pltpu.VMEM((BLOCK, BLOCK), jnp.float32),
        ],
        compiler_params=pltpu.CompilerParams(vmem_limit_bytes=VMEM_BYTES),
        cost_estimate=pl.CostEstimate(
            flops=20 * order**3, bytes_accessed=8 * order**2, transcendentals=0
        ),
        name=name,
    )(block)


def solve_kernel(blocks, side_ref, high_ref, low_ref, inv_high_ref, inv_low_ref, out_ref, kept):
    for k in range(blocks):
        here = slice(k * BLOCK, (k + 1) * BLOCK)
        total = side_ref[:, here].astype(jnp.float32)
        if k > 0:
            before = slice(0, k * BLOCK)
            total = total - contract_split(
                (out_ref[:, before], kept[:, before]), (high_ref[here, before], low_ref[here, before])
            )
        done = split(contract_split(split(total), (inv_high_ref[here, :], inv_low_ref[here, :])))
        out_ref[:, here] = done[0]
        kept[:, here] = done[1]


def solve_rows(factor_parts, side, name):
    high, low, inv_high, inv_low = factor_parts
    count, order = side.shape
    step = 256 if count % 256 == 0 else 128
    whole = pl.BlockSpec(memory_space=pltpu.VMEM)
    return pl.pallas_call(
        functools.partial(solve_kernel, order // BLOCK),
        grid=(count // step,),
        in_specs=[pl.BlockSpec((step, order), lambda i: (i, 0)), whole, whole, whole, whole],
        out_specs=pl.BlockSpec((step, order), lambda i: (i, 0)),
        out_shape=jax.ShapeDtypeStruct((count, order), jnp.bfloat16),
        scratch_shapes=[pltpu.VMEM((step, order), jnp.bfloat16)],
        compiler_params=pltpu.CompilerParams(vmem_limit_bytes=VMEM_BYTES),
        cost_estimate=pl.CostEstimate(
            flops=3 * count * order**2, bytes_accessed=8 * order**2, transcendentals=0
        ),
        name=name,
    )(side, high, low, inv_high, inv_low)


def gather_columns(block):
    rows, cols = lax.axis_size("row"), lax.axis_size("col")
    groups = cols // rows
    parts = []
    for turn in range(rows):
        pairs = []
        for h in range(rows):
            for b in range(groups):
                for i in range(rows):
                    source = h * cols + b * rows + i
                    target = ((i + turn) % rows) * cols + h * groups + b
                    pairs.append((source, target))
        parts.append(lax.ppermute(block, ("row", "col"), pairs))
    order = (lax.axis_index("row") - jnp.arange(rows)) % rows
    return jnp.take(jnp.stack(parts), order, axis=0).reshape(rows * block.shape[0], block.shape[1])


def on_device(lead, panel, row_present, trailing):
    half = lead.shape[2] // 2
    first_raw = lax.all_gather(lead[0, :, :half], "row", axis=0, tiled=True)
    panel_count = panel.shape[0]
    first_row = (lax.axis_index("row") * lax.axis_size("col") + lax.axis_index("col")) * panel_count
    tile_of = (first_row + jnp.arange(panel_count, dtype=jnp.int32)) // TILE
    tile_hits = tile_of[:, None] == jnp.arange(row_present.shape[0], dtype=jnp.int32)[None, :]
    present = jnp.sum(jnp.where(tile_hits, row_present[None, :], 0), axis=1).astype(jnp.float32)
    masked = panel * present[:, None]
    lower = lax.all_gather(lead[1], "row", axis=0, tiled=True)
    row_side = lax.all_gather(masked, "col", axis=0, tiled=True)
    col_side = gather_columns(masked)

    first = factor(first_raw, "first_factor")
    coupling = solve_rows(first, lower[:, :half], "coupling")
    schur = lower[:, half:].astype(jnp.float32) - contract(coupling, coupling)
    second = factor(schur, "second_factor")

    def panel_rows(side, name):
        first_cols = solve_rows(first, side[:, :half], name + "_first")
        remainder = side[:, half:] - contract(first_cols, coupling)
        second_cols = solve_rows(second, remainder, name + "_second")
        return jnp.concatenate([first_cols, second_cols], axis=1)

    rows_all = panel_rows(row_side, "rows")
    cols_all = panel_rows(col_side, "cols")
    updated = trailing - contract(rows_all, cols_all)
    mine = lax.axis_index("col") * panel_count
    factor_rows = lax.dynamic_slice_in_dim(rows_all, mine, panel_count, 0)
    return (updated, factor_rows)


def solution(mesh):
    in_specs = (P(None, "row", None), P(("row", "col"), None), P(), P("row", "col"))
    out_specs = (P("row", "col"), P(("row", "col"), None))
    return jax.shard_map(
        on_device, mesh=mesh, in_specs=in_specs, out_specs=out_specs, check_vma=False
    )
```

```python
import functools

import jax
import jax.numpy as jnp
from jax import lax
from jax.experimental import pallas as pl
from jax.experimental.pallas import tpu as pltpu
from jax.sharding import PartitionSpec as P

TILE = 128
BLOCK = 128
WIDE = 256
SLAB = 8
VMEM_BYTES = 48 * 1024 * 1024


def contract(left_rows, right_rows):
    return lax.dot_general(
        left_rows, right_rows, (((1,), (1,)), ((), ())), preferred_element_type=jnp.float32
    )


def split(value):
    high = value.astype(jnp.bfloat16)
    return high, (value - high.astype(jnp.float32)).astype(jnp.bfloat16)


def multiply_split(left, right):
    def multiply(x, y):
        return jnp.dot(x, y, preferred_element_type=jnp.float32)

    return (
        multiply(left[0], right[0]) + multiply(left[0], right[1]) + multiply(left[1], right[0])
    )


def contract_split(left, right):
    return (
        contract(left[0], right[0]) + contract(left[0], right[1]) + contract(left[1], right[0])
    )


def factor_block(rows, put):
    shape = (SLAB, BLOCK)
    lane = lax.broadcasted_iota(jnp.int32, shape, 1)
    sub = lax.broadcasted_iota(jnp.int32, shape, 0)

    def spread(value, row):
        return jnp.broadcast_to(value[row : row + 1, :], shape)

    rows = list(rows)
    for s in range(len(rows)):
        low = SLAB * s
        inside = (lane >= low) & (lane < low + SLAB)
        now = rows[s]
        col = [jnp.broadcast_to(now[:, low + t : low + t + 1], shape) for t in range(SLAB)]
        value = jnp.where(inside, jnp.where(lane - low == sub, 1.0, 0.0), now)
        inverse = jnp.zeros(shape, jnp.float32)
        for t in range(0, SLAB, 2):
            c0, c1 = col[t], col[t + 1]
            a, b, c = spread(c0, t), spread(c0, t + 1), spread(c1, t + 1)
            det = a * c - b * b
            over = 1.0 / det
            root_a = lax.rsqrt(a)
            root_c = lax.rsqrt(det * (root_a * root_a))
            v0, v1 = spread(value, t), spread(value, t + 1)
            second = (v1 - v0 * (b * root_a * root_a)) * root_c
            inverse = jnp.where(sub == t, v0 * root_a, jnp.where(sub == t + 1, second, inverse))
            here = (sub == t) | (sub == t + 1)
            c0 = jnp.where(sub == t, -1.0, jnp.where(sub == t + 1, 0.0, c0))
            c1 = jnp.where(sub == t, 0.0, jnp.where(sub == t + 1, -1.0, c1))
            m0 = (c0 * c - c1 * b) * over
            m1 = (c1 * a - c0 * b) * over
            for u in range(t + 2, SLAB):
                x = col[u]
                col[u] = jnp.where(here, 0.0, x) - m0 * spread(x, t) - m1 * spread(x, t + 1)
            value = jnp.where(here, 0.0, value) - m0 * v0 - m1 * v1
        put(s, jnp.where(lane <= sub + low, inverse, 0.0))
        if s + 1 < len(rows):
            lines = [spread(value, t) for t in range(SLAB)]
            for i in range(s + 1, len(rows)):
                x = rows[i]
                total = jnp.where(inside, 0.0, x)
                for t in range(SLAB):
                    total = total - jnp.broadcast_to(x[:, low + t : low + t + 1], shape) * lines[t]
                rows[i] = total


def halves(own, other, parity, index):
    first = jnp.where(parity == 0, own[index].astype(jnp.float32), other[index].astype(jnp.float32))
    last = jnp.where(parity == 0, other[index].astype(jnp.float32), own[index].astype(jnp.float32))
    return first, last


def factor_panels(held, high_ref, low_ref, inv_high_ref, inv_low_ref, inv):
    order = held.shape[0]
    for k in range(inv_high_ref.shape[0] * (WIDE // BLOCK)):
        here = slice(k * BLOCK, (k + 1) * BLOCK)
        rows = [
            held[k * BLOCK + SLAB * s : k * BLOCK + SLAB * (s + 1), here]
            for s in range(BLOCK // SLAB)
        ]

        def put(s, value):
            inv[SLAB * s : SLAB * (s + 1), :] = value

        factor_block(rows, put)
        inverse = split(inv[...])
        wide = k // 2
        top = slice(0, BLOCK)
        bottom = slice(BLOCK, 2 * BLOCK)
        if k % 2 == 0:
            earlier = inverse
            inv_high_ref[wide, top, top] = inverse[0]
            inv_low_ref[wide, top, top] = inverse[1]
            zero = jnp.zeros((BLOCK, BLOCK), jnp.bfloat16)
            inv_high_ref[wide, top, bottom] = zero
            inv_low_ref[wide, top, bottom] = zero
        else:
            inv_high_ref[wide, bottom, bottom] = inverse[0]
            inv_low_ref[wide, bottom, bottom] = inverse[1]
            left = slice((k - 1) * BLOCK, k * BLOCK)
            between = (high_ref[here, left], low_ref[here, left])
            corner = split(-multiply_split(split(multiply_split(inverse, between)), earlier))
            inv_high_ref[wide, bottom, top] = corner[0]
            inv_low_ref[wide, bottom, top] = corner[1]
        if (k + 1) * BLOCK < order:
            below = slice((k + 1) * BLOCK, order)
            factor = split(contract_split(split(held[below, here]), inverse))
            high_ref[below, here] = factor[0]
            low_ref[below, here] = factor[1]
            for j in range(k + 1, order // BLOCK):
                start = (j - k - 1) * BLOCK
                left = (factor[0][start:], factor[1][start:])
                right = (factor[0][start : start + BLOCK], factor[1][start : start + BLOCK])
                there = (slice(j * BLOCK, order), slice(j * BLOCK, (j + 1) * BLOCK))
                held[there] = held[there] - contract_split(left, right)


def beyond(source, turn, step, count):
    if step == 0:
        return source
    apart = lax.rem((source ^ turn) - source + count, count)
    return lax.rem(source + step + (apart <= step).astype(jnp.int32), count)


def pack_blocks(which, offset, count, lead_ref, sends):
    row, parity = lax.axis_index("row"), lax.rem(lax.axis_index("col"), 2)
    width = lead_ref.shape[1]
    part = width // 2
    start = pl.multiple_of(parity * part, part)
    for turn in range(1, count):
        for step in range(count // 2):
            column = beyond(row, turn, step, count) * width + offset
            column = pl.multiple_of(column, width)
            sends[turn - 1][step] = lead_ref[which, pl.ds(start, part), pl.ds(column, width)]


def pack_kernel(count, lead_ref, *sends):
    pack_blocks(0, 0, count, lead_ref, sends)


def sent_shapes(lead, count):
    width = lead.shape[1]
    return [jax.ShapeDtypeStruct((count // 2, width // 2, width), lead.dtype)] * (count - 1)


def whole_spec(shape):
    return pl.BlockSpec(shape, lambda i: (0,) * len(shape))


def pack(lead, count, half):
    shapes = sent_shapes(lead, count)
    return pl.pallas_call(
        functools.partial(pack_kernel, count),
        grid=(1,),
        in_specs=[whole_spec((1, lead.shape[1], half))],
        out_specs=[whole_spec(x.shape) for x in shapes],
        out_shape=shapes,
        name="pack",
    )(lead)


def later_kernel(count, lead_ref, panel_ref, present_ref, *rest):
    left_ref, masked_ref, *sends = rest[count - 1 :]
    part, half = left_ref.shape
    start = pl.multiple_of(lax.rem(lax.axis_index("col"), 2) * part, part)
    left_ref[...] = lead_ref[0, pl.ds(start, part), :half]
    masked_ref[...] = panel_ref[...] * present_ref[...]
    pack_blocks(0, half, count, lead_ref, sends)


def later(lead, panel, present, after):
    width, columns = lead.shape[1:]
    count = len(after) + 1
    shapes = [
        jax.ShapeDtypeStruct((width // 2, columns // 2), lead.dtype),
        jax.ShapeDtypeStruct(panel.shape, panel.dtype),
    ] + sent_shapes(lead, count)
    return pl.pallas_call(
        functools.partial(later_kernel, count),
        grid=(1,),
        in_specs=[
            pl.BlockSpec((1, width, columns), lambda i: (1, 0, 0)),
            whole_spec(panel.shape),
            whole_spec(present.shape),
        ]
        + [pl.BlockSpec(memory_space=pl.ANY)] * len(after),
        out_specs=[whole_spec(x.shape) for x in shapes],
        out_shape=shapes,
        name="later",
    )(lead, panel, present, *after)


def place_in_line(count):
    return lax.axis_index("row") if count > 1 else jnp.int32(0)


def assemble(count, slab, own, other, blocks, held):
    row, parity = place_in_line(count), lax.rem(lax.axis_index("col"), 2)
    width = held.shape[0] // count
    part = width // 2
    for turn in range(1, count):
        source = row ^ turn
        for step in range(count // 2):
            column = beyond(source, turn, step, count)
            first, last = halves(own[turn - 1], other[turn - 1], parity, step)
            blocks[source, column, :part, :] = first
            blocks[source, column, part:, :] = last
    for j in range(count):
        blocks[row, j] = slab[:, j * width : (j + 1) * width].astype(jnp.float32)
    for i in range(count):
        for j in range(i + 1):
            there = (slice(i * width, (i + 1) * width), slice(j * width, (j + 1) * width))
            if i == j:
                held[there] = blocks[i, j]
                continue
            turn = row ^ i
            have = row == i
            for step in range(1, count // 2):
                have = have | ((turn != 0) & (beyond(jnp.int32(i), turn, step, count) == j))
            have = have & (row != j)

            @pl.when(have)
            def _(there=there, i=i, j=j):
                held[there] = blocks[i, j]

            @pl.when(jnp.logical_not(have))
            def _(there=there, i=i, j=j):
                held[there] = blocks[j, i].T


def first_kernel(count, lead_ref, *refs):
    own, other = refs[: count - 1], refs[count - 1 : 2 * (count - 1)]
    outs, (blocks, held, inv) = refs[2 * (count - 1) : -3], refs[-3:]
    tail_ref, outs = outs[0], outs[1:]
    assemble(count, lead_ref.at[0], own, other, blocks, held)
    factor_panels(held, *outs, inv)
    tail_ref[...] = held[-WIDE:, -WIDE:]


def last_kernel(tail_ref, *refs):
    outs, (held, inv) = refs[:-2], refs[-2:]
    held[...] = tail_ref[...]
    factor_panels(held, *outs, inv)


def second_kernel(count, lead_ref, coupling_ref, *refs):
    own, other = refs[: count - 1], refs[count - 1 : 2 * (count - 1)]
    outs, (blocks, held, inv) = refs[2 * (count - 1) : -3], refs[-3:]
    order = held.shape[0]
    assemble(count, lead_ref.at[0], own, other, blocks, held)
    for j in range(0, order, WIDE):
        there = (slice(j, order), slice(j, j + WIDE))
        held[there] = held[there] - contract(coupling_ref[j:, :], coupling_ref[j : j + WIDE, :])
    factor_panels(held, *outs, inv)


def factor_shapes(order, done=None):
    whole = jax.ShapeDtypeStruct((order, order), jnp.bfloat16)
    inverse = jax.ShapeDtypeStruct(((done or order) // WIDE, WIDE, WIDE), jnp.bfloat16)
    return (whole, whole, inverse, inverse)


def on_chip(kernel, out_shape, scratch_shapes, flops, name, operands):
    nbytes = sum(2 * x.size for x in operands)
    return pl.pallas_call(
        kernel,
        out_shape=out_shape,
        scratch_shapes=scratch_shapes,
        compiler_params=pltpu.CompilerParams(vmem_limit_bytes=VMEM_BYTES),
        cost_estimate=pl.CostEstimate(flops=flops, bytes_accessed=nbytes, transcendentals=0),
        name=name,
    )(*operands)


def solve_step(total, k, done, kept, offset, main, last):
    high_ref, low_ref, inv_high_ref, inv_low_ref = main
    here = slice(k * WIDE, (k + 1) * WIDE)
    if k > 0:
        before = slice(0, k * WIDE)
        left = (done[:, offset : offset + k * WIDE], kept[:, before])
        total = total - contract_split(left, (high_ref[here, before], low_ref[here, before]))
    if k < inv_high_ref.shape[0]:
        inverse = (inv_high_ref[k], inv_low_ref[k])
    else:
        inverse = (last[2][0], last[3][0])
    new = split(contract_split(split(total), inverse))
    done[:, offset + k * WIDE : offset + (k + 1) * WIDE] = new[0]
    kept[:, here] = new[1]


def coupling_kernel(count, lead_ref, *refs):
    own, other = refs[: count - 1], refs[count - 1 : 2 * (count - 1)]
    main, last = refs[2 * (count - 1) :][:4], refs[2 * (count - 1) :][4:8]
    out_ref, side, kept = refs[-3:]
    row, parity = place_in_line(count), lax.rem(lax.axis_index("col"), 2)
    part, order = lead_ref.shape[1] // 2, lead_ref.shape[2]
    for turn in range(1, count):
        first, second = halves(own[turn - 1], other[turn - 1], parity, slice(None))
        start = pl.multiple_of((row ^ turn) * 2 * part, 2 * part)
        side[pl.ds(start, part), :] = first
        side[pl.ds(pl.multiple_of(start + part, part), part), :] = second
    start = pl.multiple_of(row * 2 * part, 2 * part)
    side[pl.ds(start, 2 * part), :] = lead_ref[0].astype(jnp.float32)
    for k in range(order // WIDE):
        total = side[:, k * WIDE : (k + 1) * WIDE]
        solve_step(total, k, out_ref, kept, 0, main, last)


def panel_kernel(turns, row_ref, *refs):
    parts, refs = refs[:turns], refs[turns:]
    first, last, second, refs = refs[:4], refs[4:8], refs[8:12], refs[12:]
    coupling_ref, trailing_ref, updated_ref, mine_ref, side, done, kept = refs
    row, col = lax.axis_index("row"), lax.axis_index("col")
    count, width = row_ref.shape
    piece = mine_ref.shape[0]
    half = width // 2
    side[:count, :] = row_ref[...]
    for turn in range(turns):
        place = lax.rem(row - turn + turns, turns)
        start = pl.multiple_of(count + place * piece, piece)
        side[pl.ds(start, piece), :] = parts[turn][...]
    for k in range(half // WIDE):
        solve_step(side[:, k * WIDE : (k + 1) * WIDE], k, done, kept, 0, first, last)
    for k in range(half // WIDE):
        here = slice(k * WIDE, (k + 1) * WIDE)
        total = side[:, half + k * WIDE : half + (k + 1) * WIDE]
        total = total - contract(done[:, :half], coupling_ref[here, :])
        solve_step(total, k, done, kept, half, second, None)
    updated_ref[...] = trailing_ref[...] - contract(done[:count, :], done[count:, :])
    mine_ref[...] = done[pl.ds(pl.multiple_of(col * piece, piece), piece), :]


def column_pieces(block):
    rows, cols = lax.axis_size("row"), lax.axis_size("col")
    groups = cols // rows
    parts = []
    for turn in range(rows):
        pairs = []
        for h in range(rows):
            for b in range(groups):
                for i in range(rows):
                    source = h * cols + b * rows + i
                    target = ((i + turn) % rows) * cols + h * groups + b
                    pairs.append((source, target))
        parts.append(lax.ppermute(block, ("row", "col"), pairs))
    return parts


def tie(values, after):
    return lax.optimization_barrier((values, after))[0]


def on_device(lead, panel, row_present, trailing):
    half = lead.shape[2] // 2
    rows, cols = lax.axis_size("row"), lax.axis_size("col")
    partners = [(c, c ^ 1) for c in range(cols)]
    bf16, f32 = jnp.bfloat16, jnp.float32

    def along(parts):
        return [
            lax.ppermute(part, "row", [(z, z ^ turn) for z in range(rows)])
            for turn, part in zip(range(1, rows), parts)
        ]

    def pair(parts):
        return [lax.ppermute(part, "col", partners) for part in parts]

    lines = rows
    if (half // rows) % BLOCK:
        lead = lax.all_gather(lead, "row", axis=1, tiled=True)
        lines = 1
    own = along(pack(lead, lines, half)) if lines > 1 else []
    other = pair(own)

    panel_count = panel.shape[0]
    first_row = (lax.axis_index("row") * cols + lax.axis_index("col")) * panel_count
    tile_of = (first_row + jnp.arange(panel_count, dtype=jnp.int32)) // TILE
    tile_hits = tile_of[:, None] == jnp.arange(row_present.shape[0], dtype=jnp.int32)[None, :]
    present = jnp.sum(jnp.where(tile_hits, row_present[None, :], 0), axis=1).astype(f32)
    left, masked, *right = later(lead, panel, present[:, None], own)
    left_own = along([left] * (lines - 1))
    right_own = along(right)
    row_side = lax.all_gather(masked, "col", axis=0, tiled=True)

    square = pltpu.VMEM((half, half), f32)
    block = pltpu.VMEM((BLOCK, BLOCK), f32)
    width = half // lines
    blocks = pltpu.VMEM((lines, lines, width, width), f32)

    def factor(kernel, operands, specs, shapes, scratch, name):
        return pl.pallas_call(
            kernel,
            grid=(1,),
            in_specs=specs + [whole_spec(x.shape) for x in operands[len(specs) :]],
            out_specs=[whole_spec(x.shape) for x in shapes],
            out_shape=shapes,
            scratch_shapes=scratch,
            compiler_params=pltpu.CompilerParams(vmem_limit_bytes=VMEM_BYTES),
            cost_estimate=pl.CostEstimate(
                flops=40 * half**3, bytes_accessed=8 * half**2, transcendentals=0
            ),
            name=name,
        )(*operands)

    tail_shape = jax.ShapeDtypeStruct((WIDE, WIDE), f32)
    tail, *first = factor(
        functools.partial(first_kernel, lines),
        (lead, *own, *other),
        [pl.BlockSpec((1, width, half), lambda i: (0, 0, 0))],
        (tail_shape, *factor_shapes(half, half - WIDE)),
        [blocks, square, block],
        "first_factor",
    )
    left_own = tie(left_own, tail)
    left_other = pair(left_own)
    corner = pltpu.VMEM((WIDE, WIDE), f32)
    last = factor(last_kernel, (tail,), [], factor_shapes(WIDE), [corner, block], "first_last")
    right_own = tie(right_own, last[0])
    right_other = pair(right_own)
    operands = (lead, *left_own, *left_other, *first, *last)
    coupling = factor(
        functools.partial(coupling_kernel, lines),
        operands,
        [pl.BlockSpec((1, width, half), lambda i: (1, 0, 0))],
        [jax.ShapeDtypeStruct((half, half), bf16)],
        [square, pltpu.VMEM((half, half), bf16)],
        "coupling",
    )[0]
    col_sides = column_pieces(tie(masked, coupling))
    second = factor(
        functools.partial(second_kernel, lines),
        (lead, coupling, *right_own, *right_other),
        [pl.BlockSpec((1, width, half), lambda i: (1, 0, 1))],
        factor_shapes(half),
        [blocks, square, block],
        "second_factor",
    )
    count = row_side.shape[0] + rows * panel_count
    return on_chip(
        functools.partial(panel_kernel, rows),
        (
            jax.ShapeDtypeStruct(trailing.shape, f32),
            jax.ShapeDtypeStruct(panel.shape, bf16),
        ),
        [
            pltpu.VMEM((count, 2 * half), f32),
            pltpu.VMEM((count, 2 * half), bf16),
            pltpu.VMEM((count, half), bf16),
        ],
        8 * count * half**2,
        "panel_rows",
        (row_side, *col_sides, *first, *last, *second, coupling, trailing),
    )


def solution(mesh):
    in_specs = (P(None, "row", None), P(("row", "col"), None), P(), P("row", "col"))
    out_specs = (P("row", "col"), P(("row", "col"), None))
    return jax.shard_map(
        on_device, mesh=mesh, in_specs=in_specs, out_specs=out_specs, check_vma=False
    )
```

```python
import functools

import jax
import jax.numpy as jnp
from jax import lax
from jax.experimental import pallas as pl
from jax.experimental.pallas import tpu as pltpu
from jax.sharding import PartitionSpec as P

TILE = 128
BLOCK = 128
WIDE = 256
GROUP = 8
VMEM_BYTES = 60 * 1024 * 1024


def contract(left_rows, right_rows):
    return lax.dot_general(
        left_rows, right_rows, (((1,), (1,)), ((), ())), preferred_element_type=jnp.float32
    )


def split(value):
    high = value.astype(jnp.bfloat16)
    return high, (value - high.astype(jnp.float32)).astype(jnp.bfloat16)


def multiply_split(left, right):
    def multiply(x, y):
        return jnp.dot(x, y, preferred_element_type=jnp.float32)

    return (
        multiply(left[0], right[0]) + multiply(left[0], right[1]) + multiply(left[1], right[0])
    )


def contract_split(left, right):
    return (
        contract(left[0], right[0]) + contract(left[0], right[1]) + contract(left[1], right[0])
    )


def sum_pairs(terms):
    while len(terms) > 1:
        terms = [sum(terms[i : i + 2][1:], terms[i]) for i in range(0, len(terms), 2)]
    return terms[0]


def factor_block(rows, put):
    shape = (GROUP, BLOCK)
    lane = lax.broadcasted_iota(jnp.int32, shape, 1)
    sub = lax.broadcasted_iota(jnp.int32, shape, 0)

    def spread(value, row):
        return jnp.broadcast_to(value[row : row + 1, :], shape)

    def across(value, column):
        return jnp.broadcast_to(value[:, column : column + 1], shape)

    rows = list(rows)
    count = len(rows)
    for s in range(0, count, 2):
        low = GROUP * s
        starts = [low, low + GROUP]
        within = [(lane >= x) & (lane < x + GROUP) for x in starts]
        eye = [jnp.where(lane - x == sub, 1.0, 0.0) for x in starts]
        col = [
            [across(rows[s + g], low + t) if g >= t // GROUP else None for g in range(2)]
            for t in range(2 * GROUP)
        ]
        val = [jnp.where(within[0], eye[0], rows[s]), jnp.where(within[0], 0.0, rows[s + 1])]
        corner = []
        for t in range(0, 2 * GROUP, 2):
            own, e = t // GROUP, t % GROUP
            if e == 0:
                inverse = jnp.zeros(shape, jnp.float32)
            if t == GROUP:
                corner = [across(val[0], low + GROUP + j) for j in range(GROUP)]
                val[1] = jnp.where(within[1], eye[1], val[1])
            c0, c1 = col[t], col[t + 1]
            a, b, c = spread(c0[own], e), spread(c0[own], e + 1), spread(c1[own], e + 1)
            det = a * c - b * b
            over = 1.0 / det
            here = (sub == e) | (sub == e + 1)
            v0, v1 = spread(val[own], e), spread(val[own], e + 1)
            root_a = lax.rsqrt(a)
            root_c = lax.rsqrt(det * (root_a * root_a))
            second = (v1 - v0 * (b * root_a * root_a)) * root_c
            inverse = jnp.where(sub == e, v0 * root_a, jnp.where(sub == e + 1, second, inverse))
            m0, m1 = {}, {}
            for g in range(own, 2):
                x0, x1 = c0[g], c1[g]
                if g == own:
                    x0 = jnp.where(sub == e, -1.0, jnp.where(sub == e + 1, 0.0, x0))
                    x1 = jnp.where(sub == e, 0.0, jnp.where(sub == e + 1, -1.0, x1))
                m0[g] = (x0 * c - x1 * b) * over
                m1[g] = (x1 * a - x0 * b) * over

            def step(x, g, r0, r1):
                kept = jnp.where(here, 0.0, x) if g == own else x
                return kept - (m0[g] * r0 + m1[g] * r1)

            for u in range(t + 2, 2 * GROUP):
                first, place = u // GROUP, u % GROUP
                if first == own:
                    r0, r1 = spread(col[u][own], e), spread(col[u][own], e + 1)
                else:
                    r0, r1 = spread(c0[1], place), spread(c1[1], place)
                for g in range(first, 2):
                    col[u][g] = step(col[u][g], g, r0, r1)
            for g in range(own, 2):
                val[g] = step(val[g], g, v0, v1)
            if e == GROUP - 2:
                put(s + own, jnp.where(lane <= sub + starts[own], inverse, 0.0))
        if s + 2 == count:
            return
        late = [spread(val[1], e) for e in range(GROUP)]
        top = jnp.where(within[1], 0.0, val[0])
        top = top - sum_pairs([corner[j] * late[j] for j in range(GROUP)])
        lines = [spread(top, e) for e in range(GROUP)] + late
        both = within[0] | within[1]
        for i in range(s + 2, s + 4):
            x = rows[i]
            terms = [across(x, low + t) * lines[t] for t in range(2 * GROUP)]
            rows[i] = jnp.where(both, 0.0, x) - sum_pairs(terms)
        if s + 4 < count:
            rest = jnp.concatenate(rows[s + 4 :], axis=0)
            place = lax.broadcasted_iota(jnp.int32, rest.shape, 1)
            inside = (place >= low) & (place < low + 2 * GROUP)
            zeros = [
                jnp.zeros((n, BLOCK), jnp.bfloat16) for n in (low, BLOCK - low - 2 * GROUP)
            ]
            right = [
                jnp.concatenate(([zeros[0]] if low else []) + [part, zeros[1]], axis=0)
                for part in split(jnp.concatenate([top, val[1]], axis=0))
            ]
            rest = jnp.where(inside, 0.0, rest) - multiply_split(
                split(jnp.where(inside, rest, 0.0)), right
            )
            rows[s + 4 :] = [
                rest[GROUP * j : GROUP * (j + 1), :] for j in range(count - s - 4)
            ]


class Copies:
    def __init__(self, semaphores):
        self.semaphores = semaphores
        self.used = 0

    def start(self, source, target):
        copy = pltpu.make_async_copy(source, target, self.semaphores.at[self.used])
        self.used += 1
        copy.start()
        return copy


def wait(copies):
    for copy in copies:
        copy.wait()


def factor_panels(held, done, inv, outs, copies):
    high, low, inv_high, inv_low = done
    order = held.shape[0]
    top, bottom = slice(0, BLOCK), slice(BLOCK, 2 * BLOCK)
    started = []
    for k in range(order // BLOCK):
        here = slice(k * BLOCK, (k + 1) * BLOCK)
        rows = [
            held[k * BLOCK + GROUP * s : k * BLOCK + GROUP * (s + 1), here]
            for s in range(BLOCK // GROUP)
        ]

        def put(s, value):
            inv[GROUP * s : GROUP * (s + 1), :] = value

        factor_block(rows, put)
        inverse = split(inv[...])
        wide = k // 2
        if k % 2 == 0:
            earlier = inverse
            zero = jnp.zeros((BLOCK, BLOCK), jnp.bfloat16)
            for target, part in zip((inv_high, inv_low), inverse):
                target[wide, top, top] = part
                target[wide, top, bottom] = zero
        else:
            left = slice((k - 1) * BLOCK, k * BLOCK)
            between = (high[here, left], low[here, left])
            corner = split(-multiply_split(split(multiply_split(inverse, between)), earlier))
            for target, part, side in zip((inv_high, inv_low), inverse, corner):
                target[wide, bottom, bottom] = part
                target[wide, bottom, top] = side
        if (k + 1) * BLOCK < order:
            below = slice((k + 1) * BLOCK, order)
            factor = split(contract_split(split(held[below, here]), inverse))
            high[below, here] = factor[0]
            low[below, here] = factor[1]
            for j in range(k + 1, order // BLOCK):
                start = (j - k - 1) * BLOCK
                left = (factor[0][start:], factor[1][start:])
                right = (factor[0][start : start + BLOCK], factor[1][start : start + BLOCK])
                there = (slice(j * BLOCK, order), slice(j * BLOCK, (j + 1) * BLOCK))
                held[there] = held[there] - contract_split(left, right)
        if k % 2 == 1:
            for source, target in zip(done[2:], outs[2:]):
                started.append(copies.start(source.at[wide], target.at[wide]))
            start = (k + 1) * BLOCK
            if start < order:
                there = (slice(start, order), slice(start - WIDE, start))
                for source, target in zip(done[:2], outs[:2]):
                    started.append(copies.start(source.at[there], target.at[there]))
    return started


def beyond(source, turn, step, count):
    if step == 0:
        return source
    apart = lax.rem((source ^ turn) - source + count, count)
    return lax.rem(source + step + (apart <= step).astype(jnp.int32), count)


def place_in_line(count):
    return lax.axis_index("row") if count > 1 else jnp.int32(0)


def pack_kernel(count, present_ref, lead_ref, panel_ref, masked_ref, *sends):
    row, parity = place_in_line(count), lax.rem(lax.axis_index("col"), 2)
    height = panel_ref.shape[0]
    device = lax.axis_index("row") * lax.axis_size("col") + lax.axis_index("col")
    index = lax.broadcasted_iota(jnp.int32, (height, BLOCK), 0) + device * height
    keep = jnp.zeros(index.shape, jnp.int32)
    for tile in range(present_ref.shape[0]):
        here = (index >= tile * TILE) & (index < (tile + 1) * TILE)
        keep = jnp.where(here, present_ref[tile], keep)
    keep = keep.astype(jnp.float32)
    for column in range(0, panel_ref.shape[1], BLOCK):
        there = slice(column, column + BLOCK)
        masked_ref[:, there] = panel_ref[:, there] * keep
    width, half = lead_ref.shape[1], lead_ref.shape[2] // 2
    part = width // 2
    start = pl.multiple_of(parity * part, part)
    for turn in range(1, count):
        first, second = sends[turn - 1], sends[turn + count - 2]
        second[:, :half] = lead_ref[1, pl.ds(start, part), :half]
        for step in range(count // 2):
            column = pl.multiple_of(beyond(row, turn, step, count) * width, width)
            first[step] = lead_ref[0, pl.ds(start, part), pl.ds(column, width)]
            column = pl.multiple_of(half + column, width)
            there = slice(half + step * width, half + (step + 1) * width)
            second[:, there] = lead_ref[1, pl.ds(start, part), pl.ds(column, width)]


def whole_spec(shape):
    return pl.BlockSpec(shape, lambda i: (0,) * len(shape))


def pack(lead, panel, present, count):
    width, half = lead.shape[1], lead.shape[2] // 2
    first = jax.ShapeDtypeStruct((count // 2, width // 2, width), lead.dtype)
    second = jax.ShapeDtypeStruct((width // 2, half + count // 2 * width), lead.dtype)
    shapes = [jax.ShapeDtypeStruct(panel.shape, panel.dtype)]
    shapes += [first] * (count - 1) + [second] * (count - 1)
    return pl.pallas_call(
        functools.partial(pack_kernel, count),
        grid=(1,),
        in_specs=[
            pl.BlockSpec(memory_space=pltpu.SMEM),
            whole_spec(lead.shape),
            whole_spec(panel.shape),
        ],
        out_specs=[whole_spec(x.shape) for x in shapes],
        out_shape=shapes,
        name="pack",
    )(present, lead, panel)


def fetch_blocks(count, slab, pieces, blocks, copies):
    row, parity = place_in_line(count), lax.rem(lax.axis_index("col"), 2)
    width = blocks.shape[2]
    part = width // 2
    started = []
    for j in range(count):
        started.append(copies.start(slab.at[:, j * width : (j + 1) * width], blocks.at[row, j]))
    for mine in (True, False):
        start = pl.multiple_of((parity if mine else 1 - parity) * part, part)
        for turn in range(1, count):
            source = row ^ turn
            for step in range(count // 2):
                target = blocks.at[source, beyond(source, turn, step, count), pl.ds(start, part), :]
                started.append(copies.start(pieces(turn, mine, step), target))
    return started


def lower_blocks(count, blocks, held):
    row = place_in_line(count)
    width = blocks.shape[2]
    for i in range(count):
        for j in range(i + 1):
            there = (slice(i * width, (i + 1) * width), slice(j * width, (j + 1) * width))
            if i == j:
                held[there] = blocks[i, j].astype(jnp.float32)
                continue
            turn = row ^ i
            have = row == i
            for step in range(1, count // 2):
                have = have | ((turn != 0) & (beyond(jnp.int32(i), turn, step, count) == j))
            have = have & (row != j)

            @pl.when(have)
            def _(there=there, i=i, j=j):
                held[there] = blocks[i, j].astype(jnp.float32)

            @pl.when(jnp.logical_not(have))
            def _(there=there, i=i, j=j):
                held[there] = blocks[j, i].astype(jnp.float32).T


def first_kernel(count, lead_ref, *refs):
    own, other = refs[: count - 1], refs[count - 1 : 2 * (count - 1)]
    refs = refs[2 * (count - 1) :]
    outs, (blocks, held, inv), done, semaphores = refs[:4], refs[4:7], refs[7:11], refs[11]
    copies = Copies(semaphores)
    half = held.shape[0]

    def pieces(turn, mine, step):
        return (own if mine else other)[turn - 1].at[step]

    wait(fetch_blocks(count, lead_ref.at[0, :, :half], pieces, blocks, copies))
    lower_blocks(count, blocks, held)
    wait(factor_panels(held, done, inv, outs, copies))


def solve_step(total, k, done, kept, offset, factor):
    high, low, inv_high, inv_low = factor
    here = slice(k * WIDE, (k + 1) * WIDE)
    if k > 0:
        before = slice(0, k * WIDE)
        left = (done[:, offset : offset + k * WIDE], kept[:, before])
        total = total - contract_split(left, (high[here, before], low[here, before]))
    new = split(contract_split(split(total), (inv_high[k], inv_low[k])))
    done[:, offset + k * WIDE : offset + (k + 1) * WIDE] = new[0]
    kept[:, here] = new[1]


def second_kernel(count, lead_ref, *refs):
    own, other = refs[: count - 1], refs[count - 1 : 2 * (count - 1)]
    first, refs = refs[2 * (count - 1) :][:4], refs[2 * (count - 1) + 4 :]
    coupling_ref, outs, refs = refs[0], refs[1:5], refs[5:]
    factor, (side, coupling, kept, blocks, held, inv), done, semaphores = (
        refs[:4], refs[4:10], refs[10:14], refs[14]
    )
    copies = Copies(semaphores)
    row, parity = place_in_line(count), lax.rem(lax.axis_index("col"), 2)
    half = held.shape[0]
    width = half // count
    part = width // 2

    def pieces(turn, mine, step):
        column = half + step * width
        return (own if mine else other)[turn - 1].at[:, column : column + width]

    start = pl.multiple_of(row * width, width)
    ahead = [copies.start(lead_ref.at[1, :, :half], side.at[pl.ds(start, width), :])]
    for turn in range(1, count):
        for mine in (True, False):
            start = (row ^ turn) * width + (parity if mine else 1 - parity) * part
            source = (own if mine else other)[turn - 1].at[:, :half]
            target = side.at[pl.ds(pl.multiple_of(start, part), part), :]
            ahead.append(copies.start(source, target))
    ahead += [copies.start(first[n], factor[n]) for n in (2, 3, 0, 1)]
    fetched = fetch_blocks(count, lead_ref.at[1, :, half:], pieces, blocks, copies)
    wait(ahead)
    for k in range(half // WIDE):
        total = side[:, k * WIDE : (k + 1) * WIDE].astype(jnp.float32)
        solve_step(total, k, coupling, kept, 0, factor)
    started = [copies.start(coupling, coupling_ref)]
    wait(fetched)
    lower_blocks(count, blocks, held)
    for j in range(0, half, WIDE):
        there = (slice(j, half), slice(j, j + WIDE))
        held[there] = held[there] - contract(coupling[j:, :], coupling[j : j + WIDE, :])
    started += factor_panels(held, done, inv, outs, copies)
    wait(started)


def sent_rows(piece, count):
    return pl.multiple_of(lax.rem(lax.axis_index("col"), count // piece) * piece, piece)


def row_kernel(side_ref, *refs):
    sources, (out_ref, message_ref), (side, sent, done, kept) = refs[:4], refs[4:6], refs[6:10]
    targets, semaphores = refs[10:14], refs[14]
    copies = Copies(semaphores)
    half = side.shape[1]
    fetched = [copies.start(side_ref.at[:, :half], side)]
    fetched += [copies.start(sources[n], targets[n]) for n in (2, 3, 0, 1)]
    piece = message_ref.shape[0]
    start = sent_rows(piece, side.shape[0])
    copy = copies.start(side_ref.at[pl.ds(start, piece), half:], sent)
    wait(fetched)
    for k in range(half // WIDE):
        solve_step(side[:, k * WIDE : (k + 1) * WIDE], k, done, kept, 0, targets)
    out = copies.start(done, out_ref)
    message_ref[:, :half] = done[pl.ds(start, piece), :]
    copy.wait()
    high, low = split(sent[...])
    message_ref[:, half : 2 * half] = high
    message_ref[:, 2 * half :] = low
    out.wait()


def panel_kernel(side_ref, first_ref, part_ref, *refs):
    sources, (trailing_ref, updated_ref, mine_ref) = refs[:5], refs[5:8]
    side, done, kept, message = refs[8:12]
    targets, semaphores = refs[12:17], refs[17]
    copies = Copies(semaphores)
    col = lax.axis_index("col")
    count, half = first_ref.shape
    piece = mine_ref.shape[0]
    fetched = [
        copies.start(part_ref.at[:, half:], message),
        copies.start(part_ref.at[:, :half], done.at[count:, :half]),
    ]
    fetched.append(copies.start(side_ref.at[:, half:], side.at[:count, :]))
    fetched.append(copies.start(first_ref, done.at[:count, :half]))
    fetched += [copies.start(sources[n], targets[n]) for n in (4, 2, 3, 0, 1)]
    wait(fetched)
    high, low = message[:, :half], message[:, half:]
    side[count:, :] = high.astype(jnp.float32) + low.astype(jnp.float32)
    for k in range(half // WIDE):
        here = slice(k * WIDE, (k + 1) * WIDE)
        total = side[:, here] - contract(done[:, :half], targets[4][here, :])
        solve_step(total, k, done, kept, half, targets[:4])
    updated_ref[...] = trailing_ref[...] - contract(done[:count, :], done[count:, :])
    mine_ref[...] = done[pl.ds(pl.multiple_of(col * piece, piece), piece), :]


def sender(h, r, rows):
    if rows == 4:
        return ((2, 3, 0, 1), (1, 0, 2, 3), (0, 1, 3, 2), (2, 3, 0, 1))[h][r]
    return (h + r) % rows


def to_columns(message):
    rows, cols = lax.axis_size("row"), lax.axis_size("col")
    groups = cols // rows
    pairs = [
        (h * cols + sender(h, r, rows) * groups + b, r * cols + h * groups + b)
        for h in range(rows)
        for r in range(rows)
        for b in range(groups)
    ]
    return lax.ppermute(message, ("row", "col"), pairs)


def tie(values, after):
    return lax.optimization_barrier((values, after))[0]


def on_device(lead, panel, row_present, trailing):
    half = lead.shape[2] // 2
    rows, cols = lax.axis_size("row"), lax.axis_size("col")
    partners = [(c, c ^ 1) for c in range(cols)]
    bf16, f32 = jnp.bfloat16, jnp.float32

    def along(parts):
        return [
            lax.ppermute(part, "row", [(z, z ^ turn) for z in range(rows)])
            for turn, part in zip(range(1, rows), parts)
        ]

    def pair(parts):
        return [lax.ppermute(part, "col", partners) for part in parts]

    lines = rows
    if (half // rows) % BLOCK:
        lead = lax.all_gather(lead, "row", axis=1, tiled=True)
        lines = 1
    panel_count = panel.shape[0]
    masked, *sends = pack(lead, panel, row_present, lines)
    row_side = lax.all_gather(masked, "col", axis=0, tiled=True)
    own = along(sends[: lines - 1])
    other = pair(own)
    second_sends = sends[lines - 1 :]
    second_sends = [tie(x, y) for x, y in zip(second_sends, own)]
    second_own = along(second_sends)

    square, square16 = pltpu.VMEM((half, half), f32), pltpu.VMEM((half, half), bf16)
    block = pltpu.VMEM((BLOCK, BLOCK), f32)
    width = half // lines
    blocks = pltpu.VMEM((lines, lines, width, width), bf16)
    whole = jax.ShapeDtypeStruct((half, half), bf16)
    inverse = jax.ShapeDtypeStruct((half // WIDE, WIDE, WIDE), bf16)
    factor = (whole, whole, inverse, inverse)
    factor_scratch = [pltpu.VMEM(x.shape, bf16) for x in factor]
    hbm, vmem = pl.BlockSpec(memory_space=pltpu.HBM), pl.BlockSpec(memory_space=pltpu.VMEM)

    def call(kernel, operands, in_specs, shapes, out_specs, scratch, semaphores, name, **other):
        return pl.pallas_call(
            kernel,
            in_specs=in_specs,
            out_specs=out_specs,
            out_shape=shapes,
            scratch_shapes=scratch + [pltpu.SemaphoreType.DMA((semaphores,))],
            compiler_params=pltpu.CompilerParams(vmem_limit_bytes=VMEM_BYTES),
            cost_estimate=pl.CostEstimate(
                flops=40 * half**3, bytes_accessed=8 * half**2, transcendentals=0
            ),
            name=name,
            **other,
        )(*operands)

    wides = half // WIDE
    sent = (lines - 1) * lines + lines
    operands = (lead, *own, *other)
    first = call(
        functools.partial(first_kernel, lines),
        operands,
        [hbm] * len(operands),
        factor,
        [hbm] * 4,
        [blocks, square, block, *factor_scratch],
        sent + 4 * wides,
        "first_factor",
    )
    if lines > 1:
        second_own = tie(second_own, first)
    second_other = pair(second_own)
    count = row_side.shape[0]
    rows_first, message = call(
        row_kernel,
        (row_side, *first),
        [hbm] * 5,
        (
            jax.ShapeDtypeStruct((count, half), bf16),
            jax.ShapeDtypeStruct((count * rows // cols, 3 * half), bf16),
        ),
        [hbm, vmem],
        [
            pltpu.VMEM((count, half), f32),
            pltpu.VMEM((count * rows // cols, half), f32),
            pltpu.VMEM((count, half), bf16),
            pltpu.VMEM((count, half), bf16),
            *factor_scratch,
        ],
        7,
        "row_first",
    )
    message = to_columns(message)
    operands = (lead, *second_own, *second_other, *first)
    coupling, *second = call(
        functools.partial(second_kernel, lines),
        operands,
        [hbm] * len(operands),
        (whole, *factor),
        [hbm] * 5,
        factor_scratch + [square16, square16, square16, blocks, square, block] + factor_scratch,
        2 * (lines - 1) + 6 + sent + 4 * wides,
        "second_factor",
    )
    count = count + rows * panel_count
    operands = (row_side, rows_first, message, *second, coupling, trailing)
    return call(
        panel_kernel,
        operands,
        [hbm] * (len(operands) - 1) + [vmem],
        (
            jax.ShapeDtypeStruct(trailing.shape, f32),
            jax.ShapeDtypeStruct(panel.shape, bf16),
        ),
        [vmem] * 2,
        [
            pltpu.VMEM((count, half), f32),
            pltpu.VMEM((count, 2 * half), bf16),
            pltpu.VMEM((count, half), bf16),
            pltpu.VMEM((rows * panel_count, 2 * half), bf16),
            *factor_scratch,
            square16,
        ],
        9,
        "panel_rows",
    )


def solution(mesh):
    in_specs = (P(None, "row", None), P(("row", "col"), None), P(), P("row", "col"))
    out_specs = (P("row", "col"), P(("row", "col"), None))
    return jax.shard_map(
        on_device, mesh=mesh, in_specs=in_specs, out_specs=out_specs, check_vma=False
    )
```

```python
import functools

import jax
import jax.numpy as jnp
from jax import lax
from jax.experimental import pallas as pl
from jax.experimental.pallas import tpu as pltpu
from jax.sharding import PartitionSpec as P

TILE = 128
VMEM_BYTES = 60 * 1024 * 1024
BLOCK = 128
WIDE = 256
GROUP = 8


def contract(left_rows, right_rows):
    return lax.dot_general(
        left_rows, right_rows, (((1,), (1,)), ((), ())), preferred_element_type=jnp.float32
    )


def split(value):
    high = value.astype(jnp.bfloat16)
    return high, (value - high.astype(jnp.float32)).astype(jnp.bfloat16)


def multiply_split(left, right):
    return jnp.dot(
        jnp.concatenate([left[0], left[0], left[1]], axis=1),
        jnp.concatenate([right[0], right[1], right[0]], axis=0),
        preferred_element_type=jnp.float32,
    )


def contract_split(left, right):
    return contract(
        jnp.concatenate([left[0], left[0], left[1]], axis=1),
        jnp.concatenate([right[0], right[1], right[0]], axis=1),
    )


def sum_pairs(terms):
    while len(terms) > 1:
        terms = [sum(terms[i : i + 2][1:], terms[i]) for i in range(0, len(terms), 2)]
    return terms[0]


def factor_block(rows, put):
    shape = (GROUP, BLOCK)
    lane = lax.broadcasted_iota(jnp.int32, shape, 1)
    sub = lax.broadcasted_iota(jnp.int32, shape, 0)

    def spread(value, row):
        return jnp.broadcast_to(value[row : row + 1, :], shape)

    def across(value, column):
        return jnp.broadcast_to(value[:, column : column + 1], shape)

    rows = list(rows)
    count = len(rows)
    for s in range(0, count, 2):
        low = GROUP * s
        starts = [low, low + GROUP]
        within = [(lane >= x) & (lane < x + GROUP) for x in starts]
        eye = [jnp.where(lane - x == sub, 1.0, 0.0) for x in starts]
        col = [
            [across(rows[s + g], low + t) if g >= t // GROUP else None for g in range(2)]
            for t in range(2 * GROUP)
        ]
        val = [jnp.where(within[0], eye[0], rows[s]), jnp.where(within[0], 0.0, rows[s + 1])]
        corner = []
        for t in range(0, 2 * GROUP, 2):
            own, e = t // GROUP, t % GROUP
            if e == 0:
                inverse = jnp.zeros(shape, jnp.float32)
            if t == GROUP:
                corner = [across(val[0], low + GROUP + j) for j in range(GROUP)]
                val[1] = jnp.where(within[1], eye[1], val[1])
            c0, c1 = col[t], col[t + 1]
            a, b, c = spread(c0[own], e), spread(c0[own], e + 1), spread(c1[own], e + 1)
            det = a * c - b * b
            over = 1.0 / det
            here = (sub == e) | (sub == e + 1)
            v0, v1 = spread(val[own], e), spread(val[own], e + 1)
            root_a = lax.rsqrt(a)
            root_c = lax.rsqrt(det * (root_a * root_a))
            second = (v1 - v0 * (b * root_a * root_a)) * root_c
            inverse = jnp.where(sub == e, v0 * root_a, jnp.where(sub == e + 1, second, inverse))
            m0, m1 = {}, {}
            for g in range(own, 2):
                x0, x1 = c0[g], c1[g]
                if g == own:
                    x0 = jnp.where(sub == e, -1.0, jnp.where(sub == e + 1, 0.0, x0))
                    x1 = jnp.where(sub == e, 0.0, jnp.where(sub == e + 1, -1.0, x1))
                m0[g] = (x0 * c - x1 * b) * over
                m1[g] = (x1 * a - x0 * b) * over

            def step(x, g, r0, r1):
                kept = jnp.where(here, 0.0, x) if g == own else x
                return kept - (m0[g] * r0 + m1[g] * r1)

            for u in range(t + 2, 2 * GROUP):
                first, place = u // GROUP, u % GROUP
                if first == own:
                    r0, r1 = spread(col[u][own], e), spread(col[u][own], e + 1)
                else:
                    r0, r1 = spread(c0[1], place), spread(c1[1], place)
                for g in range(first, 2):
                    col[u][g] = step(col[u][g], g, r0, r1)
            for g in range(own, 2):
                val[g] = step(val[g], g, v0, v1)
            if e == GROUP - 2:
                put(s + own, jnp.where(lane <= sub + starts[own], inverse, 0.0))
        if s + 2 == count:
            return
        late = [spread(val[1], e) for e in range(GROUP)]
        top = jnp.where(within[1], 0.0, val[0])
        top = top - sum_pairs([corner[j] * late[j] for j in range(GROUP)])
        lines = [spread(top, e) for e in range(GROUP)] + late
        both = within[0] | within[1]
        for i in range(s + 2, s + 4):
            x = rows[i]
            terms = [across(x, low + t) * lines[t] for t in range(2 * GROUP)]
            rows[i] = jnp.where(both, 0.0, x) - sum_pairs(terms)
        if s + 4 < count:
            rest = jnp.concatenate(rows[s + 4 :], axis=0)
            place = lax.broadcasted_iota(jnp.int32, rest.shape, 1)
            inside = (place >= low) & (place < low + 2 * GROUP)
            zeros = [
                jnp.zeros((n, BLOCK), jnp.bfloat16) for n in (low, BLOCK - low - 2 * GROUP)
            ]
            right = [
                jnp.concatenate(([zeros[0]] if low else []) + [part, zeros[1]], axis=0)
                for part in split(jnp.concatenate([top, val[1]], axis=0))
            ]
            rest = jnp.where(inside, 0.0, rest) - multiply_split(
                split(jnp.where(inside, rest, 0.0)), right
            )
            rows[s + 4 :] = [
                rest[GROUP * j : GROUP * (j + 1), :] for j in range(count - s - 4)
            ]


class Copies:
    def __init__(self, semaphores):
        self.semaphores = semaphores
        self.used = 0

    def start(self, source, target):
        copy = pltpu.make_async_copy(source, target, self.semaphores.at[self.used])
        self.used += 1
        copy.start()
        return copy


def wait(copies):
    for copy in copies:
        copy.wait()


def factor_panels(held, done, inv, outs, copies):
    high, low, inv_high, inv_low = done
    order = held.shape[0]
    top, bottom = slice(0, BLOCK), slice(BLOCK, 2 * BLOCK)
    started = []
    for k in range(order // BLOCK):
        here = slice(k * BLOCK, (k + 1) * BLOCK)
        rows = [
            held[k * BLOCK + GROUP * s : k * BLOCK + GROUP * (s + 1), here]
            for s in range(BLOCK // GROUP)
        ]

        def put(s, value):
            inv[GROUP * s : GROUP * (s + 1), :] = value

        factor_block(rows, put)
        inverse = split(inv[...])
        wide = k // 2
        if k % 2 == 0:
            earlier = inverse
            zero = jnp.zeros((BLOCK, BLOCK), jnp.bfloat16)
            for target, part in zip((inv_high, inv_low), inverse):
                target[wide, top, top] = part
                target[wide, top, bottom] = zero
        else:
            left = slice((k - 1) * BLOCK, k * BLOCK)
            between = (high[here, left], low[here, left])
            corner = split(-multiply_split(split(multiply_split(inverse, between)), earlier))
            for target, part, side in zip((inv_high, inv_low), inverse, corner):
                target[wide, bottom, bottom] = part
                target[wide, bottom, top] = side
        if (k + 1) * BLOCK < order:
            below = slice((k + 1) * BLOCK, order)
            factor = split(contract_split(split(held[below, here]), inverse))
            high[below, here] = factor[0]
            low[below, here] = factor[1]
            for j in range(k + 1, order // BLOCK):
                start = (j - k - 1) * BLOCK
                left = (factor[0][start:], factor[1][start:])
                right = (factor[0][start : start + BLOCK], factor[1][start : start + BLOCK])
                there = (slice(j * BLOCK, order), slice(j * BLOCK, (j + 1) * BLOCK))
                held[there] = held[there] - contract_split(left, right)
        if k % 2 == 1:
            for source, target in zip(done[2:], outs[2:]):
                started.append(copies.start(source.at[wide], target.at[wide]))
            start = (k + 1) * BLOCK
            if start < order:
                there = (slice(start, order), slice(start - WIDE, start))
                for source, target in zip(done[:2], outs[:2]):
                    started.append(copies.start(source.at[there], target.at[there]))
    return started


def beyond(source, turn, step, count):
    if step == 0:
        return source
    apart = lax.rem((source ^ turn) - source + count, count)
    return lax.rem(source + step + (apart <= step).astype(jnp.int32), count)


def place_in_line(count):
    return lax.axis_index("row") if count > 1 else jnp.int32(0)


def without(skipped, step):
    return step + (skipped <= step).astype(jnp.int32)


def pack_kernel(count, present_ref, lead_ref, panel_ref, masked_ref, *sends):
    row, parity = place_in_line(count), lax.rem(lax.axis_index("col"), 2)
    height = panel_ref.shape[0]
    device = lax.axis_index("row") * lax.axis_size("col") + lax.axis_index("col")
    index = lax.broadcasted_iota(jnp.int32, (height, BLOCK), 0) + device * height
    keep = jnp.zeros(index.shape, jnp.int32)
    for tile in range(present_ref.shape[0]):
        here = (index >= tile * TILE) & (index < (tile + 1) * TILE)
        keep = jnp.where(here, present_ref[tile], keep)
    keep = keep.astype(jnp.float32)
    for column in range(0, panel_ref.shape[1], BLOCK):
        there = slice(column, column + BLOCK)
        masked_ref[:, there] = panel_ref[:, there] * keep
    width, half = lead_ref.shape[1], lead_ref.shape[2] // 2
    part = width // 2
    start = pl.multiple_of(parity * part, part)
    for turn in range(1, count):
        first, second = sends[turn - 1], sends[turn + count - 2]
        for step in range(count - 1):
            column = pl.multiple_of(without(row ^ turn, step) * width, width)
            there = slice(step * width, (step + 1) * width)
            second[:, there] = lead_ref[1, pl.ds(start, part), pl.ds(column, width)]
        for step in range(count // 2):
            column = pl.multiple_of(beyond(row, turn, step, count) * width, width)
            first[step] = lead_ref[0, pl.ds(start, part), pl.ds(column, width)]
            column = pl.multiple_of(half + column, width)
            there = slice((count - 1 + step) * width, (count + step) * width)
            second[:, there] = lead_ref[1, pl.ds(start, part), pl.ds(column, width)]


def whole_spec(shape):
    return pl.BlockSpec(shape, lambda i: (0,) * len(shape))


def pack(lead, panel, present, count):
    width = lead.shape[1]
    first = jax.ShapeDtypeStruct((count // 2, width // 2, width), lead.dtype)
    second = jax.ShapeDtypeStruct((width // 2, (count - 1 + count // 2) * width), lead.dtype)
    shapes = [jax.ShapeDtypeStruct(panel.shape, panel.dtype)]
    shapes += [first] * (count - 1) + [second] * (count - 1)
    return pl.pallas_call(
        functools.partial(pack_kernel, count),
        grid=(1,),
        in_specs=[
            pl.BlockSpec(memory_space=pltpu.SMEM),
            whole_spec(lead.shape),
            whole_spec(panel.shape),
        ],
        out_specs=[whole_spec(x.shape) for x in shapes],
        out_shape=shapes,
        name="pack",
    )(present, lead, panel)


def fetch_blocks(count, slab, pieces, blocks, copies):
    row, parity = place_in_line(count), lax.rem(lax.axis_index("col"), 2)
    width = blocks.shape[2]
    part = width // 2
    started = []
    for j in range(count):
        started.append(copies.start(slab.at[:, j * width : (j + 1) * width], blocks.at[row, j]))
    for mine in (True, False):
        start = pl.multiple_of((parity if mine else 1 - parity) * part, part)
        for turn in range(1, count):
            source = row ^ turn
            for step in range(count // 2):
                target = blocks.at[source, beyond(source, turn, step, count), pl.ds(start, part), :]
                started.append(copies.start(pieces(turn, mine, step), target))
    return started


def lower_blocks(count, blocks, held):
    row = place_in_line(count)
    width = blocks.shape[2]
    for i in range(count):
        for j in range(i + 1):
            there = (slice(i * width, (i + 1) * width), slice(j * width, (j + 1) * width))
            if i == j:
                held[there] = blocks[i, j].astype(jnp.float32)
                continue
            turn = row ^ i
            have = row == i
            for step in range(1, count // 2):
                have = have | ((turn != 0) & (beyond(jnp.int32(i), turn, step, count) == j))
            have = have & (row != j)

            @pl.when(have)
            def _(there=there, i=i, j=j):
                held[there] = blocks[i, j].astype(jnp.float32)

            @pl.when(jnp.logical_not(have))
            def _(there=there, i=i, j=j):
                held[there] = blocks[j, i].astype(jnp.float32).T


def first_kernel(count, lead_ref, *refs):
    own, other = refs[: count - 1], refs[count - 1 : 2 * (count - 1)]
    refs = refs[2 * (count - 1) :]
    outs, (blocks, held, inv), done, semaphores = refs[:4], refs[4:7], refs[7:11], refs[11]
    copies = Copies(semaphores)
    half = held.shape[0]

    def pieces(turn, mine, step):
        return (own if mine else other)[turn - 1].at[step]

    wait(fetch_blocks(count, lead_ref.at[0, :, :half], pieces, blocks, copies))
    lower_blocks(count, blocks, held)
    wait(factor_panels(held, done, inv, outs, copies))


def solve_step(total, k, done, kept, offset, factor):
    high, low, inv_high, inv_low = factor
    here = slice(k * WIDE, (k + 1) * WIDE)
    if k > 0:
        before = slice(0, k * WIDE)
        left = (done[:, offset : offset + k * WIDE], kept[:, before])
        total = total - contract_split(left, (high[here, before], low[here, before]))
    new = split(contract_split(split(total), (inv_high[k], inv_low[k])))
    done[:, offset + k * WIDE : offset + (k + 1) * WIDE] = new[0]
    kept[:, here] = new[1]


def second_kernel(count, lead_ref, *refs):
    own, other = refs[: count - 1], refs[count - 1 : 2 * (count - 1)]
    first, refs = refs[2 * (count - 1) :][:4], refs[2 * (count - 1) + 4 :]
    coupling_ref, outs, refs = refs[0], refs[1:5], refs[5:]
    factor, (side, coupling, kept, blocks, held, inv, across), done, semaphores = (
        refs[:4], refs[4:11], refs[11:15], refs[15]
    )
    copies = Copies(semaphores)
    row, parity = place_in_line(count), lax.rem(lax.axis_index("col"), 2)
    half = held.shape[0]
    width = half // count
    part = width // 2

    def pieces(turn, mine, step):
        column = (count - 1 + step) * width
        return (own if mine else other)[turn - 1].at[:, column : column + width]

    start = pl.multiple_of(row * width, width)
    ahead = [copies.start(lead_ref.at[1, :, :half], side.at[pl.ds(start, width), :])]
    ahead.append(copies.start(lead_ref.at[0, :, half:], across))
    ahead += [copies.start(first[n], factor[n]) for n in (2, 3)]
    for turn in range(1, count):
        for mine in (True, False):
            start = (row ^ turn) * width + (parity if mine else 1 - parity) * part
            start = pl.multiple_of(start, part)
            source = (own if mine else other)[turn - 1]
            for step in range(count - 1):
                column = pl.multiple_of(without(row, step) * width, width)
                target = side.at[pl.ds(start, part), pl.ds(column, width)]
                ahead.append(
                    copies.start(source.at[:, step * width : (step + 1) * width], target)
                )
    below = [copies.start(first[n], factor[n]) for n in (0, 1)]
    fetched = fetch_blocks(count, lead_ref.at[1, :, half:], pieces, blocks, copies)
    wait(ahead)
    if count > 1:
        column = pl.multiple_of(row * width, width)
        for j in range(count):
            there = slice(j * width, (j + 1) * width)
            turned = across[:, there].astype(jnp.float32).T.astype(side.dtype)
            side[there, pl.ds(column, width)] = turned
    for k in range(half // WIDE):
        if k == 1:
            wait(below)
        total = side[:, k * WIDE : (k + 1) * WIDE].astype(jnp.float32)
        solve_step(total, k, coupling, kept, 0, factor)
    started = [copies.start(coupling, coupling_ref)]
    wait(fetched)
    lower_blocks(count, blocks, held)
    for j in range(0, half, WIDE):
        there = (slice(j, half), slice(j, j + WIDE))
        held[there] = held[there] - contract(coupling[j:, :], coupling[j : j + WIDE, :])
    started += factor_panels(held, done, inv, outs, copies)
    wait(started)


def sent_rows(piece, count):
    return pl.multiple_of(lax.rem(lax.axis_index("col"), count // piece) * piece, piece)


def row_kernel(side_ref, *refs):
    sources, (out_ref, message_ref), (side, sent, done, kept) = refs[:4], refs[4:6], refs[6:10]
    targets, semaphores = refs[10:14], refs[14]
    copies = Copies(semaphores)
    half = side.shape[1]
    fetched = [copies.start(side_ref.at[:, :half], side)]
    fetched += [copies.start(sources[n], targets[n]) for n in (2, 3)]
    below = [copies.start(sources[n], targets[n]) for n in (0, 1)]
    piece = message_ref.shape[0]
    start = sent_rows(piece, side.shape[0])
    copy = copies.start(side_ref.at[pl.ds(start, piece), half:], sent)
    wait(fetched)
    for k in range(half // WIDE):
        if k == 1:
            wait(below)
        solve_step(side[:, k * WIDE : (k + 1) * WIDE], k, done, kept, 0, targets)
    out = copies.start(done, out_ref)
    message_ref[:, :half] = done[pl.ds(start, piece), :]
    copy.wait()
    high, low = split(sent[...])
    message_ref[:, half : 2 * half] = high
    message_ref[:, 2 * half :] = low
    out.wait()


def panel_kernel(side_ref, first_ref, part_ref, *refs):
    sources, (trailing_ref, updated_ref, mine_ref) = refs[:5], refs[5:8]
    side, done, kept, message = refs[8:12]
    targets, semaphores = refs[12:17], refs[17]
    copies = Copies(semaphores)
    col = lax.axis_index("col")
    count, half = first_ref.shape
    piece = mine_ref.shape[0]
    fetched = [
        copies.start(part_ref.at[:, half:], message),
        copies.start(part_ref.at[:, :half], done.at[count:, :half]),
    ]
    fetched.append(copies.start(side_ref.at[:, half:], side.at[:count, :]))
    fetched.append(copies.start(first_ref, done.at[:count, :half]))
    fetched += [copies.start(sources[n], targets[n]) for n in (4, 2, 3)]
    below = [copies.start(sources[n], targets[n]) for n in (0, 1)]
    wait(fetched)
    high, low = message[:, :half], message[:, half:]
    side[count:, :] = high.astype(jnp.float32) + low.astype(jnp.float32)
    for k in range(half // WIDE):
        if k == 1:
            wait(below)
        here = slice(k * WIDE, (k + 1) * WIDE)
        total = side[:, here] - contract(done[:, :half], targets[4][here, :])
        solve_step(total, k, done, kept, half, targets[:4])
    updated_ref[...] = trailing_ref[...] - contract(done[:count, :], done[count:, :])
    mine_ref[...] = done[pl.ds(pl.multiple_of(col * piece, piece), piece), :]


def sender(h, r, rows):
    if rows == 4:
        return ((2, 3, 0, 1), (1, 0, 2, 3), (0, 1, 3, 2), (2, 3, 0, 1))[h][r]
    return (h + r) % rows


def to_columns(message):
    rows, cols = lax.axis_size("row"), lax.axis_size("col")
    groups = cols // rows
    pairs = [
        (h * cols + sender(h, r, rows) * groups + b, r * cols + h * groups + b)
        for h in range(rows)
        for r in range(rows)
        for b in range(groups)
    ]
    return lax.ppermute(message, ("row", "col"), pairs)


def tie(values, after):
    return lax.optimization_barrier((values, after))[0]


def on_device(lead, panel, row_present, trailing):
    half = lead.shape[2] // 2
    rows, cols = lax.axis_size("row"), lax.axis_size("col")
    partners = [(c, c ^ 1) for c in range(cols)]
    bf16, f32 = jnp.bfloat16, jnp.float32

    def along(parts):
        return [
            lax.ppermute(part, "row", [(z, z ^ turn) for z in range(rows)])
            for turn, part in zip(range(1, rows), parts)
        ]

    def pair(parts):
        return [lax.ppermute(part, "col", partners) for part in parts]

    lines = rows
    if (half // rows) % BLOCK:
        lead = lax.all_gather(lead, "row", axis=1, tiled=True)
        lines = 1
    panel_count = panel.shape[0]
    masked, *sends = pack(lead, panel, row_present, lines)
    row_side = lax.all_gather(masked, "col", axis=0, tiled=True)
    own = along(sends[: lines - 1])
    other = pair(own)
    second_sends = sends[lines - 1 :]
    second_sends = [tie(x, y) for x, y in zip(second_sends, own)]
    second_own = along(second_sends)

    square, square16 = pltpu.VMEM((half, half), f32), pltpu.VMEM((half, half), bf16)
    block = pltpu.VMEM((BLOCK, BLOCK), f32)
    width = half // lines
    blocks = pltpu.VMEM((lines, lines, width, width), bf16)
    whole = jax.ShapeDtypeStruct((half, half), bf16)
    inverse = jax.ShapeDtypeStruct((half // WIDE, WIDE, WIDE), bf16)
    factor = (whole, whole, inverse, inverse)
    factor_scratch = [pltpu.VMEM(x.shape, bf16) for x in factor]
    hbm, vmem = pl.BlockSpec(memory_space=pltpu.HBM), pl.BlockSpec(memory_space=pltpu.VMEM)

    def call(kernel, operands, in_specs, shapes, out_specs, scratch, semaphores, name):
        return pl.pallas_call(
            kernel,
            in_specs=in_specs,
            out_specs=out_specs,
            out_shape=shapes,
            scratch_shapes=scratch + [pltpu.SemaphoreType.DMA((semaphores,))],
            compiler_params=pltpu.CompilerParams(vmem_limit_bytes=VMEM_BYTES),
            cost_estimate=pl.CostEstimate(
                flops=40 * half**3, bytes_accessed=8 * half**2, transcendentals=0
            ),
            name=name,
        )(*operands)

    wides = half // WIDE
    sent = (lines - 1) * lines + lines
    operands = (lead, *own, *other)
    first = call(
        functools.partial(first_kernel, lines),
        operands,
        [hbm] * len(operands),
        factor,
        [hbm] * 4,
        [blocks, square, block, *factor_scratch],
        sent + 4 * wides,
        "first_factor",
    )
    if lines > 1:
        second_own = tie(second_own, first)
    second_other = pair(second_own)
    count = row_side.shape[0]
    rows_first, message = call(
        row_kernel,
        (row_side, *first),
        [hbm] * 5,
        (
            jax.ShapeDtypeStruct((count, half), bf16),
            jax.ShapeDtypeStruct((count * rows // cols, 3 * half), bf16),
        ),
        [hbm, vmem],
        [
            pltpu.VMEM((count, half), f32),
            pltpu.VMEM((count * rows // cols, half), f32),
            pltpu.VMEM((count, half), bf16),
            pltpu.VMEM((count, half), bf16),
            *factor_scratch,
        ],
        7,
        "row_first",
    )
    message = to_columns(message)
    operands = (lead, *second_own, *second_other, *first)
    coupling, *second = call(
        functools.partial(second_kernel, lines),
        operands,
        [hbm] * len(operands),
        (whole, *factor),
        [hbm] * 5,
        factor_scratch
        + [square16, square16, square16, blocks, square, block]
        + [pltpu.VMEM((width, half), bf16)]
        + factor_scratch,
        2 * (lines - 1) ** 2 + 7 + sent + 4 * wides,
        "second_factor",
    )
    count = count + rows * panel_count
    operands = (row_side, rows_first, message, *second, coupling, trailing)
    return call(
        panel_kernel,
        operands,
        [hbm] * (len(operands) - 1) + [vmem],
        (
            jax.ShapeDtypeStruct(trailing.shape, f32),
            jax.ShapeDtypeStruct(panel.shape, bf16),
        ),
        [vmem] * 2,
        [
            pltpu.VMEM((count, half), f32),
            pltpu.VMEM((count, 2 * half), bf16),
            pltpu.VMEM((count, half), bf16),
            pltpu.VMEM((rows * panel_count, 2 * half), bf16),
            *factor_scratch,
            square16,
        ],
        9,
        "panel_rows",
    )


def solution(mesh):
    in_specs = (P(None, "row", None), P(("row", "col"), None), P(), P("row", "col"))
    out_specs = (P("row", "col"), P(("row", "col"), None))
    return jax.shard_map(
        on_device, mesh=mesh, in_specs=in_specs, out_specs=out_specs, check_vma=False
    )
```

```python
import functools

import jax
import jax.numpy as jnp
from jax import lax
from jax.experimental import pallas as pl
from jax.experimental.pallas import tpu as pltpu
from jax.sharding import PartitionSpec as P

TILE = 128
VMEM_BYTES = 63 * 1024 * 1024
BLOCK = 128
WIDE = 256
GROUP = 8


def contract(left_rows, right_rows):
    return lax.dot_general(
        left_rows, right_rows, (((1,), (1,)), ((), ())), preferred_element_type=jnp.float32
    )


def split(value):
    high = value.astype(jnp.bfloat16)
    return high, (value - high.astype(jnp.float32)).astype(jnp.bfloat16)


def multiply_split(left, right):
    return jnp.dot(
        jnp.concatenate([left[0], left[0], left[1]], axis=1),
        jnp.concatenate([right[0], right[1], right[0]], axis=0),
        preferred_element_type=jnp.float32,
    )


def contract_split(left, right):
    return contract(
        jnp.concatenate([left[0], left[0], left[1]], axis=1),
        jnp.concatenate([right[0], right[1], right[0]], axis=1),
    )


def sum_pairs(terms):
    while len(terms) > 1:
        terms = [sum(terms[i : i + 2][1:], terms[i]) for i in range(0, len(terms), 2)]
    return terms[0]


def factor_block(rows, put):
    shape = (GROUP, BLOCK)
    lane = lax.broadcasted_iota(jnp.int32, shape, 1)
    sub = lax.broadcasted_iota(jnp.int32, shape, 0)

    def spread(value, row):
        return jnp.broadcast_to(value[row : row + 1, :], shape)

    def across(value, column):
        return jnp.broadcast_to(value[:, column : column + 1], shape)

    rows = list(rows)
    count = len(rows)
    for s in range(0, count, 2):
        low = GROUP * s
        starts = [low, low + GROUP]
        within = [(lane >= x) & (lane < x + GROUP) for x in starts]
        eye = [jnp.where(lane - x == sub, 1.0, 0.0) for x in starts]
        col = [
            [across(rows[s + g], low + t) if g >= t // GROUP else None for g in range(2)]
            for t in range(2 * GROUP)
        ]
        val = [jnp.where(within[0], eye[0], rows[s]), jnp.where(within[0], 0.0, rows[s + 1])]
        corner = []
        for t in range(0, 2 * GROUP, 2):
            own, e = t // GROUP, t % GROUP
            if e == 0:
                inverse = jnp.zeros(shape, jnp.float32)
            if t == GROUP:
                corner = [across(val[0], low + GROUP + j) for j in range(GROUP)]
                val[1] = jnp.where(within[1], eye[1], val[1])
            c0, c1 = col[t], col[t + 1]
            a, b, c = spread(c0[own], e), spread(c0[own], e + 1), spread(c1[own], e + 1)
            det = a * c - b * b
            over = 1.0 / det
            here = (sub == e) | (sub == e + 1)
            v0, v1 = spread(val[own], e), spread(val[own], e + 1)
            root_a = lax.rsqrt(a)
            root_c = lax.rsqrt(det * (root_a * root_a))
            second = (v1 - v0 * (b * root_a * root_a)) * root_c
            inverse = jnp.where(sub == e, v0 * root_a, jnp.where(sub == e + 1, second, inverse))
            m0, m1 = {}, {}
            for g in range(own, 2):
                x0, x1 = c0[g], c1[g]
                if g == own:
                    x0 = jnp.where(sub == e, -1.0, jnp.where(sub == e + 1, 0.0, x0))
                    x1 = jnp.where(sub == e, 0.0, jnp.where(sub == e + 1, -1.0, x1))
                m0[g] = (x0 * c - x1 * b) * over
                m1[g] = (x1 * a - x0 * b) * over

            def step(x, g, r0, r1):
                kept = jnp.where(here, 0.0, x) if g == own else x
                return kept - (m0[g] * r0 + m1[g] * r1)

            for u in range(t + 2, 2 * GROUP):
                first, place = u // GROUP, u % GROUP
                if first == own:
                    r0, r1 = spread(col[u][own], e), spread(col[u][own], e + 1)
                else:
                    r0, r1 = spread(c0[1], place), spread(c1[1], place)
                for g in range(first, 2):
                    col[u][g] = step(col[u][g], g, r0, r1)
            for g in range(own, 2):
                val[g] = step(val[g], g, v0, v1)
            if e == GROUP - 2:
                put(s + own, jnp.where(lane <= sub + starts[own], inverse, 0.0))
        if s + 2 == count:
            return
        late = [spread(val[1], e) for e in range(GROUP)]
        top = jnp.where(within[1], 0.0, val[0])
        top = top - sum_pairs([corner[j] * late[j] for j in range(GROUP)])
        lines = [spread(top, e) for e in range(GROUP)] + late
        both = within[0] | within[1]
        for i in range(s + 2, s + 4):
            x = rows[i]
            terms = [across(x, low + t) * lines[t] for t in range(2 * GROUP)]
            rows[i] = jnp.where(both, 0.0, x) - sum_pairs(terms)
        if s + 4 < count:
            rest = jnp.concatenate(rows[s + 4 :], axis=0)
            place = lax.broadcasted_iota(jnp.int32, rest.shape, 1)
            inside = (place >= low) & (place < low + 2 * GROUP)
            zeros = [
                jnp.zeros((n, BLOCK), jnp.bfloat16) for n in (low, BLOCK - low - 2 * GROUP)
            ]
            right = [
                jnp.concatenate(([zeros[0]] if low else []) + [part, zeros[1]], axis=0)
                for part in split(jnp.concatenate([top, val[1]], axis=0))
            ]
            rest = jnp.where(inside, 0.0, rest) - multiply_split(
                split(jnp.where(inside, rest, 0.0)), right
            )
            rows[s + 4 :] = [
                rest[GROUP * j : GROUP * (j + 1), :] for j in range(count - s - 4)
            ]


class Copies:
    def __init__(self, semaphores):
        self.semaphores = semaphores
        self.used = 0

    def start(self, source, target):
        copy = pltpu.make_async_copy(source, target, self.semaphores.at[self.used])
        self.used += 1
        copy.start()
        return copy


def wait(copies):
    for copy in copies:
        copy.wait()


def factor_panels(held, done, inv, outs, copies):
    high, low, inv_high, inv_low = done
    order = held.shape[0]
    top, bottom = slice(0, BLOCK), slice(BLOCK, 2 * BLOCK)
    started = []
    for k in range(order // BLOCK):
        here = slice(k * BLOCK, (k + 1) * BLOCK)
        rows = [
            held[k * BLOCK + GROUP * s : k * BLOCK + GROUP * (s + 1), here]
            for s in range(BLOCK // GROUP)
        ]

        def put(s, value):
            inv[GROUP * s : GROUP * (s + 1), :] = value

        factor_block(rows, put)
        inverse = split(inv[...])
        wide = k // 2
        if k % 2 == 0:
            earlier = inverse
            zero = jnp.zeros((BLOCK, BLOCK), jnp.bfloat16)
            for target, part in zip((inv_high, inv_low), inverse):
                target[wide, top, top] = part
                target[wide, top, bottom] = zero
        else:
            left = slice((k - 1) * BLOCK, k * BLOCK)
            between = (high[here, left], low[here, left])
            corner = split(-multiply_split(split(multiply_split(inverse, between)), earlier))
            for target, part, side in zip((inv_high, inv_low), inverse, corner):
                target[wide, bottom, bottom] = part
                target[wide, bottom, top] = side
        if (k + 1) * BLOCK < order:
            below = slice((k + 1) * BLOCK, order)
            factor = split(contract_split(split(held[below, here]), inverse))
            high[below, here] = factor[0]
            low[below, here] = factor[1]
            for j in range(k + 1, order // BLOCK):
                start = (j - k - 1) * BLOCK
                left = (factor[0][start:], factor[1][start:])
                right = (factor[0][start : start + BLOCK], factor[1][start : start + BLOCK])
                there = (slice(j * BLOCK, order), slice(j * BLOCK, (j + 1) * BLOCK))
                held[there] = held[there] - contract_split(left, right)
        if k % 2 == 1:
            for source, target in zip(done[2:], outs[2:]):
                started.append(copies.start(source.at[wide], target.at[wide]))
            start = (k + 1) * BLOCK
            if start < order:
                there = (slice(start, order), slice(start - WIDE, start))
                for source, target in zip(done[:2], outs[:2]):
                    started.append(copies.start(source.at[there], target.at[there]))
    return started


def beyond(source, turn, step, count):
    if step == 0:
        return source
    apart = lax.rem((source ^ turn) - source + count, count)
    return lax.rem(source + step + (apart <= step).astype(jnp.int32), count)


def place_in_line(count):
    return lax.axis_index("row") if count > 1 else jnp.int32(0)


def without(skipped, step):
    return step + (skipped <= step).astype(jnp.int32)


def pack_kernel(count, present_ref, lead_ref, panel_ref, masked_ref, *sends):
    row, parity = place_in_line(count), lax.rem(lax.axis_index("col"), 2)
    height = panel_ref.shape[0]
    device = lax.axis_index("row") * lax.axis_size("col") + lax.axis_index("col")
    index = lax.broadcasted_iota(jnp.int32, (height, BLOCK), 0) + device * height
    keep = jnp.zeros(index.shape, jnp.int32)
    for tile in range(present_ref.shape[0]):
        here = (index >= tile * TILE) & (index < (tile + 1) * TILE)
        keep = jnp.where(here, present_ref[tile], keep)
    keep = keep.astype(jnp.float32)
    for column in range(0, panel_ref.shape[1], BLOCK):
        there = slice(column, column + BLOCK)
        masked_ref[:, there] = panel_ref[:, there] * keep
    width, half = lead_ref.shape[1], lead_ref.shape[2] // 2
    part = width // 2
    start = pl.multiple_of(parity * part, part)
    for turn in range(1, count):
        first, second = sends[turn - 1], sends[turn + count - 2]
        for step in range(count - 1):
            column = pl.multiple_of(without(row ^ turn, step) * width, width)
            there = slice(step * width, (step + 1) * width)
            second[:, there] = lead_ref[1, pl.ds(start, part), pl.ds(column, width)]
        for step in range(count // 2):
            column = pl.multiple_of(beyond(row, turn, step, count) * width, width)
            first[step] = lead_ref[0, pl.ds(start, part), pl.ds(column, width)]
            column = pl.multiple_of(half + column, width)
            there = slice((count - 1 + step) * width, (count + step) * width)
            second[:, there] = lead_ref[1, pl.ds(start, part), pl.ds(column, width)]


def whole_spec(shape):
    return pl.BlockSpec(shape, lambda i: (0,) * len(shape))


def pack(lead, panel, present, count):
    width = lead.shape[1]
    first = jax.ShapeDtypeStruct((count // 2, width // 2, width), lead.dtype)
    second = jax.ShapeDtypeStruct((width // 2, (count - 1 + count // 2) * width), lead.dtype)
    shapes = [jax.ShapeDtypeStruct(panel.shape, panel.dtype)]
    shapes += [first] * (count - 1) + [second] * (count - 1)
    return pl.pallas_call(
        functools.partial(pack_kernel, count),
        grid=(1,),
        in_specs=[
            pl.BlockSpec(memory_space=pltpu.SMEM),
            whole_spec(lead.shape),
            whole_spec(panel.shape),
        ],
        out_specs=[whole_spec(x.shape) for x in shapes],
        out_shape=shapes,
        name="pack",
    )(present, lead, panel)


def fetch_blocks(count, slab, pieces, blocks, copies):
    row, parity = place_in_line(count), lax.rem(lax.axis_index("col"), 2)
    width = blocks.shape[2]
    part = width // 2
    started = []
    for j in range(count):
        started.append(copies.start(slab.at[:, j * width : (j + 1) * width], blocks.at[row, j]))
    for mine in (True, False):
        start = pl.multiple_of((parity if mine else 1 - parity) * part, part)
        for turn in range(1, count):
            source = row ^ turn
            for step in range(count // 2):
                target = blocks.at[source, beyond(source, turn, step, count), pl.ds(start, part), :]
                started.append(copies.start(pieces(turn, mine, step), target))
    return started


def lower_blocks(count, blocks, held):
    row = place_in_line(count)
    width = blocks.shape[2]
    for i in range(count):
        for j in range(i + 1):
            there = (slice(i * width, (i + 1) * width), slice(j * width, (j + 1) * width))
            if i == j:
                held[there] = blocks[i, j].astype(jnp.float32)
                continue
            turn = row ^ i
            have = row == i
            for step in range(1, count // 2):
                have = have | ((turn != 0) & (beyond(jnp.int32(i), turn, step, count) == j))
            have = have & (row != j)

            @pl.when(have)
            def _(there=there, i=i, j=j):
                held[there] = blocks[i, j].astype(jnp.float32)

            @pl.when(jnp.logical_not(have))
            def _(there=there, i=i, j=j):
                held[there] = blocks[j, i].astype(jnp.float32).T


def first_kernel(count, lead_ref, *refs):
    own, other = refs[: count - 1], refs[count - 1 : 2 * (count - 1)]
    refs = refs[2 * (count - 1) :]
    outs, (blocks, held, inv), done, semaphores = refs[:4], refs[4:7], refs[7:11], refs[11]
    copies = Copies(semaphores)
    half = held.shape[0]

    def pieces(turn, mine, step):
        return (own if mine else other)[turn - 1].at[step]

    wait(fetch_blocks(count, lead_ref.at[0, :, :half], pieces, blocks, copies))
    lower_blocks(count, blocks, held)
    wait(factor_panels(held, done, inv, outs, copies))


def fetch_factor(k, sources, targets, copies):
    here = slice(k * WIDE, (k + 1) * WIDE)
    started = [copies.start(sources[n].at[k], targets[n].at[k]) for n in (2, 3)]
    if k > 0:
        there = (here, slice(0, k * WIDE))
        started += [copies.start(sources[n].at[there], targets[n].at[there]) for n in (0, 1)]
    return started


def solve_step(total, k, done, kept, offset, factor):
    high, low, inv_high, inv_low = factor
    here = slice(k * WIDE, (k + 1) * WIDE)
    if k > 0:
        before = slice(0, k * WIDE)
        left = (done[:, offset : offset + k * WIDE], kept[:, before])
        total = total - contract_split(left, (high[here, before], low[here, before]))
    new = split(contract_split(split(total), (inv_high[k], inv_low[k])))
    done[:, offset + k * WIDE : offset + (k + 1) * WIDE] = new[0]
    kept[:, here] = new[1]


def second_kernel(count, lead_ref, *refs):
    own, other = refs[: count - 1], refs[count - 1 : 2 * (count - 1)]
    first, refs = refs[2 * (count - 1) :][:4], refs[2 * (count - 1) + 4 :]
    coupling_ref, outs, refs = refs[0], refs[1:5], refs[5:]
    factor, (side, coupling, kept, blocks, held, inv, across), done, semaphores = (
        refs[:4], refs[4:11], refs[11:15], refs[15]
    )
    copies = Copies(semaphores)
    row, parity = place_in_line(count), lax.rem(lax.axis_index("col"), 2)
    half = held.shape[0]
    width = half // count
    part = width // 2

    def pieces(turn, mine, step):
        column = (count - 1 + step) * width
        return (own if mine else other)[turn - 1].at[:, column : column + width]

    start = pl.multiple_of(row * width, width)
    ahead = [copies.start(lead_ref.at[1, :, :half], side.at[pl.ds(start, width), :])]
    ahead.append(copies.start(lead_ref.at[0, :, half:], across))
    for turn in range(1, count):
        for mine in (True, False):
            start = (row ^ turn) * width + (parity if mine else 1 - parity) * part
            start = pl.multiple_of(start, part)
            source = (own if mine else other)[turn - 1]
            for step in range(count - 1):
                column = pl.multiple_of(without(row, step) * width, width)
                target = side.at[pl.ds(start, part), pl.ds(column, width)]
                ahead.append(
                    copies.start(source.at[:, step * width : (step + 1) * width], target)
                )
    needed = [fetch_factor(k, first, factor, copies) for k in range(half // WIDE)]
    fetched = fetch_blocks(count, lead_ref.at[1, :, half:], pieces, blocks, copies)
    wait(ahead)
    if count > 1:
        column = pl.multiple_of(row * width, width)
        for j in range(count):
            there = slice(j * width, (j + 1) * width)
            turned = across[:, there].astype(jnp.float32).T.astype(side.dtype)
            side[there, pl.ds(column, width)] = turned
    for k in range(half // WIDE):
        wait(needed[k])
        total = side[:, k * WIDE : (k + 1) * WIDE].astype(jnp.float32)
        solve_step(total, k, coupling, kept, 0, factor)
    started = [copies.start(coupling, coupling_ref)]
    wait(fetched)
    lower_blocks(count, blocks, held)
    for j in range(0, half, WIDE):
        there = (slice(j, half), slice(j, j + WIDE))
        held[there] = held[there] - contract(coupling[j:, :], coupling[j : j + WIDE, :])
    started += factor_panels(held, done, inv, outs, copies)
    wait(started)


def sent_rows(piece, count):
    return pl.multiple_of(lax.rem(lax.axis_index("col"), count // piece) * piece, piece)


def row_kernel(side_ref, *refs):
    sources, (out_ref, message_ref), (side, sent, done, kept) = refs[:4], refs[4:6], refs[6:10]
    targets, semaphores = refs[10:14], refs[14]
    copies = Copies(semaphores)
    half = side.shape[1]
    needed = []
    for k in range(half // WIDE):
        here = slice(k * WIDE, (k + 1) * WIDE)
        needed.append([copies.start(side_ref.at[:, here], side.at[:, here])])
        needed[k] += fetch_factor(k, sources, targets, copies)
    piece = message_ref.shape[0]
    start = sent_rows(piece, side.shape[0])
    copy = copies.start(side_ref.at[pl.ds(start, piece), half:], sent)
    for k in range(half // WIDE):
        wait(needed[k])
        solve_step(side[:, k * WIDE : (k + 1) * WIDE], k, done, kept, 0, targets)
    out = copies.start(done, out_ref)
    message_ref[:, :half] = done[pl.ds(start, piece), :]
    copy.wait()
    high, low = split(sent[...])
    message_ref[:, half : 2 * half] = high
    message_ref[:, 2 * half :] = low
    out.wait()


def panel_kernel(side_ref, first_ref, part_ref, *refs):
    sources, (trailing_ref, updated_ref, mine_ref) = refs[:5], refs[5:8]
    side, done, kept, message = refs[8:12]
    targets, semaphores = refs[12:17], refs[17]
    copies = Copies(semaphores)
    col = lax.axis_index("col")
    count, half = first_ref.shape
    piece = mine_ref.shape[0]
    fetched = [
        copies.start(part_ref.at[:, half:], message),
        copies.start(part_ref.at[:, :half], done.at[count:, :half]),
    ]
    fetched.append(copies.start(first_ref, done.at[:count, :half]))
    for k in range(half // WIDE):
        here = slice(k * WIDE, (k + 1) * WIDE)
        there = slice(half + k * WIDE, half + (k + 1) * WIDE)
        needed = [copies.start(sources[4].at[here, :], targets[4].at[here, :])]
        needed.append(copies.start(side_ref.at[:, there], side.at[:count, here]))
        needed += fetch_factor(k, sources, targets, copies)
        fetched.append(needed)
    wait(fetched[:3])
    for k in range(half // WIDE):
        wait(fetched[3 + k])
        here = slice(k * WIDE, (k + 1) * WIDE)
        there = slice(half + k * WIDE, half + (k + 1) * WIDE)
        side[count:, here] = message[:, here].astype(jnp.float32) + message[:, there].astype(
            jnp.float32
        )
        total = side[:, here] - contract(done[:, :half], targets[4][here, :])
        solve_step(total, k, done, kept, half, targets[:4])
    updated_ref[...] = trailing_ref[...] - contract(done[:count, :], done[count:, :])
    mine_ref[...] = done[pl.ds(pl.multiple_of(col * piece, piece), piece), :]


def sender(h, r, rows):
    if rows == 4:
        return ((2, 3, 0, 1), (1, 0, 2, 3), (0, 1, 3, 2), (2, 3, 0, 1))[h][r]
    return (h + r) % rows


def to_columns(message):
    rows, cols = lax.axis_size("row"), lax.axis_size("col")
    groups = cols // rows
    pairs = [
        (h * cols + sender(h, r, rows) * groups + b, r * cols + h * groups + b)
        for h in range(rows)
        for r in range(rows)
        for b in range(groups)
    ]
    return lax.ppermute(message, ("row", "col"), pairs)


def tie(values, after):
    return lax.optimization_barrier((values, after))[0]


def on_device(lead, panel, row_present, trailing):
    half = lead.shape[2] // 2
    rows, cols = lax.axis_size("row"), lax.axis_size("col")
    partners = [(c, c ^ 1) for c in range(cols)]
    bf16, f32 = jnp.bfloat16, jnp.float32

    def along(parts):
        return [
            lax.ppermute(part, "row", [(z, z ^ turn) for z in range(rows)])
            for turn, part in zip(range(1, rows), parts)
        ]

    def pair(parts):
        return [lax.ppermute(part, "col", partners) for part in parts]

    lines = rows
    if (half // rows) % BLOCK:
        lead = lax.all_gather(lead, "row", axis=1, tiled=True)
        lines = 1
    panel_count = panel.shape[0]
    masked, *sends = pack(lead, panel, row_present, lines)
    row_side = lax.all_gather(masked, "col", axis=0, tiled=True)
    own = along(sends[: lines - 1])
    other = pair(own)
    second_sends = sends[lines - 1 :]
    second_sends = [tie(x, y) for x, y in zip(second_sends, own)]
    second_own = along(second_sends)

    square, square16 = pltpu.VMEM((half, half), f32), pltpu.VMEM((half, half), bf16)
    block = pltpu.VMEM((BLOCK, BLOCK), f32)
    width = half // lines
    blocks = pltpu.VMEM((lines, lines, width, width), bf16)
    whole = jax.ShapeDtypeStruct((half, half), bf16)
    inverse = jax.ShapeDtypeStruct((half // WIDE, WIDE, WIDE), bf16)
    factor = (whole, whole, inverse, inverse)
    factor_scratch = [pltpu.VMEM(x.shape, bf16) for x in factor]
    hbm, vmem = pl.BlockSpec(memory_space=pltpu.HBM), pl.BlockSpec(memory_space=pltpu.VMEM)

    def call(kernel, operands, in_specs, shapes, out_specs, scratch, semaphores, name):
        return pl.pallas_call(
            kernel,
            in_specs=in_specs,
            out_specs=out_specs,
            out_shape=shapes,
            scratch_shapes=scratch + [pltpu.SemaphoreType.DMA((semaphores,))],
            compiler_params=pltpu.CompilerParams(vmem_limit_bytes=VMEM_BYTES),
            cost_estimate=pl.CostEstimate(
                flops=40 * half**3, bytes_accessed=8 * half**2, transcendentals=0
            ),
            name=name,
        )(*operands)

    wides = half // WIDE
    sent = (lines - 1) * lines + lines
    operands = (lead, *own, *other)
    first = call(
        functools.partial(first_kernel, lines),
        operands,
        [hbm] * len(operands),
        factor,
        [hbm] * 4,
        [blocks, square, block, *factor_scratch],
        sent + 4 * wides,
        "first_factor",
    )
    if lines > 1:
        second_own = tie(second_own, first)
    second_other = pair(second_own)
    count = row_side.shape[0]
    rows_first, message = call(
        row_kernel,
        (row_side, *first),
        [hbm] * 5,
        (
            jax.ShapeDtypeStruct((count, half), bf16),
            jax.ShapeDtypeStruct((count * rows // cols, 3 * half), bf16),
        ),
        [hbm, vmem],
        [
            pltpu.VMEM((count, half), f32),
            pltpu.VMEM((count * rows // cols, half), f32),
            pltpu.VMEM((count, half), bf16),
            pltpu.VMEM((count, half), bf16),
            *factor_scratch,
        ],
        5 * wides + 2,
        "row_first",
    )
    message = to_columns(message)
    operands = (lead, *second_own, *second_other, *first)
    coupling, *second = call(
        functools.partial(second_kernel, lines),
        operands,
        [hbm] * len(operands),
        (whole, *factor),
        [hbm] * 5,
        factor_scratch
        + [square16, square16, square16, blocks, square, block]
        + [pltpu.VMEM((width, half), bf16)]
        + factor_scratch,
        2 * (lines - 1) ** 2 + 3 + sent + 8 * wides,
        "second_factor",
    )
    count = count + rows * panel_count
    operands = (row_side, rows_first, message, *second, coupling, trailing)
    return call(
        panel_kernel,
        operands,
        [hbm] * (len(operands) - 1) + [vmem],
        (
            jax.ShapeDtypeStruct(trailing.shape, f32),
            jax.ShapeDtypeStruct(panel.shape, bf16),
        ),
        [vmem] * 2,
        [
            pltpu.VMEM((count, half), f32),
            pltpu.VMEM((count, 2 * half), bf16),
            pltpu.VMEM((count, half), bf16),
            pltpu.VMEM((rows * panel_count, 2 * half), bf16),
            *factor_scratch,
            square16,
        ],
        6 * wides + 3,
        "panel_rows",
    )


def solution(mesh):
    in_specs = (P(None, "row", None), P(("row", "col"), None), P(), P("row", "col"))
    out_specs = (P("row", "col"), P(("row", "col"), None))
    return jax.shard_map(
        on_device, mesh=mesh, in_specs=in_specs, out_specs=out_specs, check_vma=False
    )
```
